512 devices in a mesh: seq: 32 (over x, z_hi, core), col: 16 (over y, z_lo).
Axes of the slice: x: 4, y: 4, z: 16 (z_hi: 4, z_lo: 4; z = z_hi * 4 + z_lo), core: 2. Of those that a mesh axis runs over, the one named last changes fastest.
Arguments:
- alignment_embedding_tensor: bfloat16 [512, 128, 768], P('seq', 'col'), may hold values from -3 to 3
- horizontal_attention_triples: bfloat16 [512, 128, 2304], P('seq', 'col'), may hold values from -10 to 10
- occupancy_indicator: int32 [512, 128], P('seq', 'col'), may hold values from 0 to 1, as said below
- horizontal_attention_exit_matrix: bfloat16 [768, 768], P('col'), may hold values from -0.21875 to 0.21875
- vertical_attention_entry_matrix: bfloat16 [768, 2304], P('col'), may hold values from -0.43164062 to 0.43164062
- vertical_attention_exit_matrix: bfloat16 [768, 768], P('col'), may hold values from -0.21875 to 0.21875
- vertical_layernorm_scaling: float32 [768], replicated, may hold values from 0.25 to 1.75
Outputs:
- mixed: float32 [512, 128, 768], P('seq', 'col')
The draws below stay inside these ranges and needn't reach their ends.
Inputs may be any that keep to these rules, and one draw needn't show every extreme that they name: `occupancy_indicator`: every column holds a residue in some sequence.
All inputs are finite; a program needn't handle non-finite values.
Results may differ from the reference program's by a relative error of at most 0.035.
Values may be sent and summed in bfloat16 or wider, within the bound.
A program may use at most 64 MiB of HBM per device.

```python
import math
import jax
import jax.numpy as jnp
from jax import lax

EMBED_DIMENSION = 768
H = 12
DH = 64
ALIGNED_PROTEINS = 512
ALIGNED_SITES = 128


def draw_horizontal_attention_triples(key, part):
    base = jnp.clip(jax.random.normal(key, (ALIGNED_PROTEINS, ALIGNED_SITES, 3 * EMBED_DIMENSION), jnp.float32), -5.5, 5.5)
    factor = jnp.concatenate((jnp.full((2 * EMBED_DIMENSION,), 1.7, jnp.float32), jnp.full((EMBED_DIMENSION,), 1.8, jnp.float32)))
    base = base * factor[None, None, :]
    base = jnp.clip(base, -10.0, 10.0)
    return base.astype(jnp.bfloat16)


def draw_occupancy_indicator(key, part):
    first, second, third, fourth, fifth = jax.random.split(jax.random.fold_in(key, 5), 5)
    start = jax.random.randint(first, (ALIGNED_PROTEINS, 1), ALIGNED_SITES // 3, ALIGNED_SITES // 2)
    length_unit = jax.random.randint(second, (ALIGNED_PROTEINS, 1), 0, ALIGNED_SITES // 16 + 1)
    boost = jnp.repeat(jax.random.randint(third, (ALIGNED_PROTEINS // 8, 1), 1, 5), 8, axis=0)
    length = length_unit * boost
    column = jnp.arange(ALIGNED_SITES, dtype=jnp.int32)[None, :]
    band = (column >= start) & (column < start + length)
    scattered = jax.random.randint(fourth, (ALIGNED_PROTEINS, ALIGNED_SITES), 0, 20) == 0
    keeper = jnp.repeat(jax.random.randint(fifth, (ALIGNED_PROTEINS // 8,), 0, 8), 8)
    keep_row = jnp.arange(ALIGNED_PROTEINS, dtype=jnp.int32) % 8 == keeper
    gap = (band | scattered) & jnp.logical_not(keep_row)[:, None]
    return jnp.where(gap, 0, 1).astype(jnp.int32)


def steps_of(own_key, extent, cuts, smallest, high):
    def one(dim, blocks):
        steps = jax.random.uniform(jax.random.fold_in(jax.random.fold_in(own_key, 6), dim), (blocks,), jnp.float32, smallest / len(cuts), high / len(cuts))
        return jnp.repeat(jnp.exp(steps), extent[dim] // blocks).reshape((-1,) + (1,) * (len(extent) - dim - 1))

    level = one(*cuts[0])
    for cut in cuts[1:]:
        level = level * one(*cut)
    return level


def normal_values(rng, extent, spread, limit, cuts=(), held_as=jnp.bfloat16):
    result = jax.random.normal(rng, extent, jnp.float32) * spread
    if len(cuts) > 0:
        result = steps_of(rng, extent, cuts, -0.22, 0.18) * result
    return jnp.clip(result, min=-limit, max=limit).astype(held_as)


def setup_inputs(seed: int = 0) -> dict:
    arg_keys = jax.random.split(jax.random.key(seed), 8)
    alignment_embedding_tensor = normal_values(arg_keys[0], (ALIGNED_PROTEINS, ALIGNED_SITES, EMBED_DIMENSION), 0.5, 3.0, ((0, 32), (1, 16)))
    horizontal_attention_triples = draw_horizontal_attention_triples(jax.random.fold_in(arg_keys[7], 71), 0)
    occupancy_indicator = draw_occupancy_indicator(jax.random.fold_in(arg_keys[7], 71), 0)
    horizontal_attention_exit_matrix = normal_values(arg_keys[3], (EMBED_DIMENSION, EMBED_DIMENSION), EMBED_DIMENSION ** -0.5, 0.21875, ((0, 16),))
    vertical_attention_entry_matrix = normal_values(arg_keys[4], (EMBED_DIMENSION, 3 * EMBED_DIMENSION), (2.0 / EMBED_DIMENSION ** 0.5), 0.43164062, ((0, 16),))
    vertical_attention_exit_matrix = normal_values(arg_keys[5], (EMBED_DIMENSION, EMBED_DIMENSION), EMBED_DIMENSION ** -0.5, 0.21875, ((0, 16),))
    vertical_layernorm_scaling = jnp.clip(1.0 + 0.15 * jax.random.normal(arg_keys[6], (EMBED_DIMENSION,), jnp.float32), 0.25, 1.75)
    return {"alignment_embedding_tensor": alignment_embedding_tensor, "horizontal_attention_triples": horizontal_attention_triples, "occupancy_indicator": occupancy_indicator, "horizontal_attention_exit_matrix": horizontal_attention_exit_matrix, "vertical_attention_entry_matrix": vertical_attention_entry_matrix, "vertical_attention_exit_matrix": vertical_attention_exit_matrix, "vertical_layernorm_scaling": vertical_layernorm_scaling}


def reference(alignment_embedding_tensor, horizontal_attention_triples, occupancy_indicator, horizontal_attention_exit_matrix, vertical_attention_entry_matrix, vertical_attention_exit_matrix, vertical_layernorm_scaling):
    live = occupancy_indicator.astype(jnp.float32)
    parts = horizontal_attention_triples.reshape(ALIGNED_PROTEINS, ALIGNED_SITES, 3, H, DH).astype(jnp.float32)
    query = parts[:, :, 0] * live[:, :, None, None]
    keys = parts[:, :, 1]
    values = parts[:, :, 2]
    scale = 1.0 / (math.sqrt(DH) * math.sqrt(ALIGNED_PROTEINS))
    logits = jnp.einsum('rihd,rjhd->hij', query, keys) * scale
    row_probs = jax.nn.softmax(logits, axis=-1).astype(jnp.bfloat16)
    row_context = jnp.einsum('hij,rjhd->rihd', row_probs.astype(jnp.float32), values).astype(jnp.bfloat16)
    merged_attended_heads = row_context.reshape(ALIGNED_PROTEINS * ALIGNED_SITES, EMBED_DIMENSION)
    skip_connection_hidden = alignment_embedding_tensor.reshape(ALIGNED_PROTEINS * ALIGNED_SITES, EMBED_DIMENSION).astype(jnp.float32) + jnp.dot(merged_attended_heads, horizontal_attention_exit_matrix, preferred_element_type=jnp.float32)
    center = skip_connection_hidden - lax.optimization_barrier(jnp.mean(skip_connection_hidden, axis=-1, keepdims=True))
    variance = lax.optimization_barrier(jnp.mean(center * center, axis=-1, keepdims=True))
    normed = (center * lax.rsqrt(variance + 1e-05) * vertical_layernorm_scaling).astype(jnp.bfloat16)
    col_qkv = jnp.dot(normed, vertical_attention_entry_matrix, preferred_element_type=jnp.float32).astype(jnp.bfloat16)
    col_qkv = col_qkv.reshape(ALIGNED_PROTEINS, ALIGNED_SITES, 3, H, DH)
    per_column = jnp.transpose(col_qkv, (1, 0, 2, 3, 4))
    live_columns = jnp.transpose(live, (1, 0))

    def attend(pieces):
        block, keep = pieces
        cq = block[:, 0].astype(jnp.float32)
        ck = block[:, 1].astype(jnp.float32)
        cv = block[:, 2].astype(jnp.float32)
        scores = jnp.einsum('rhd,shd->hrs', cq, ck) / math.sqrt(DH)
        scores = jnp.where(keep[None, None, :] > 0, scores, -1000000000.0)
        probs = jax.nn.softmax(scores, axis=-1).astype(jnp.bfloat16)
        return jnp.einsum('hrs,shd->rhd', probs.astype(jnp.float32), cv).astype(jnp.bfloat16)
    col_context = lax.map(attend, (per_column, live_columns))
    col_context = jnp.transpose(col_context, (1, 0, 2, 3)).reshape(ALIGNED_PROTEINS * ALIGNED_SITES, EMBED_DIMENSION)
    mixed = skip_connection_hidden + jnp.dot(col_context, vertical_attention_exit_matrix, preferred_element_type=jnp.float32)
    return mixed.reshape(ALIGNED_PROTEINS, ALIGNED_SITES, EMBED_DIMENSION)
```

```python
import functools
import math

import jax
import jax.numpy as jnp
from jax import lax
from jax.experimental import pallas as pl
from jax.experimental.pallas import tpu as pltpu
from jax.sharding import Mesh
from jax.sharding import PartitionSpec as P

H = 12
DH = 64
F32 = jnp.float32
BF16 = jnp.bfloat16
MESH = pl.DeviceIdType.MESH


class Links:
    def __init__(self, send_sem, recv_sem):
        self.send_sem, self.recv_sem, self.count, self.started = send_sem, recv_sem, 0, []

    def copy(self, src, dst, device):
        k = self.count
        self.count += 1
        made = pltpu.make_async_remote_copy(
            src_ref=src,
            dst_ref=dst,
            send_sem=self.send_sem.at[k],
            recv_sem=self.recv_sem.at[k],
            device_id=device,
            device_id_type=MESH,
        )
        made.start()
        self.started.append(made)
        return made

    def finish(self):
        for made in self.started:
            made.wait_send()


class Place:
    def __init__(self):
        s, c = lax.axis_index("seq"), lax.axis_index("col")
        self.x, self.zh, self.co = s // 8, (s // 2) % 4, s % 2
        self.y, self.zl = c // 4, c % 4

    def at(self, **moved):
        g = {k: moved.get(k, getattr(self, k)) for k in ("x", "zh", "co", "y", "zl")}
        return (g["x"] * 8 + g["zh"] * 2 + g["co"], g["y"] * 4 + g["zl"])

    def group(self):
        return self.x * 2 + self.co

    def in_group(self, d):
        g = (self.group() + d) % 8
        return g, self.at(x=g // 2, co=g % 2)

    def cousin(self):
        return self.zh * 2 + self.zl % 2

    def in_cousins(self, d):
        e = (self.cousin() + d) % 8
        return e, self.at(zh=e // 2, zl=(self.zl // 2) * 2 + e % 2)


def meet(devices):
    barrier = pltpu.get_barrier_semaphore()
    for device in devices:
        pl.semaphore_signal(barrier, inc=1, device_id=device, device_id_type=MESH)
    pl.semaphore_wait(barrier, len(devices))


def row_kernel(
    trip, occ, out, qs, kbuf, vbuf, qbuf, lsend, lrecv, erecv, pbuf, csend, crecv, send_sem, recv_sem
):
    me = Place()
    links = Links(send_sem, recv_sem)
    along_z = [((me.zl + d) % 4, me.at(zl=(me.zl + d) % 4)) for d in range(1, 4)]
    up, down = me.at(y=(me.y + 1) % 4), me.at(y=(me.y + 3) % 4)
    y_up, y_down = (me.y + 1) % 4, (me.y + 3) % 4
    cousins = []
    for zh in range(1, 4):
        for other in range(2):
            cousins.append(
                me.at(zh=(me.zh + zh) % 4, zl=(me.zl // 2) * 2 + (me.zl + other) % 2)
            )
    everyone = [d for _, d in along_z] + [up, down] + [me.in_group(d)[1] for d in range(1, 8)] + cousins

    rows = lax.broadcasted_iota(jnp.int32, (128, 16), 0)
    seqs = lax.broadcasted_iota(jnp.int32, (128, 16), 1)
    spread = jnp.dot(
        (rows // 8 == seqs).astype(BF16), occ[...].astype(F32).astype(BF16), preferred_element_type=F32
    )
    picked = lax.broadcasted_iota(jnp.int32, (128, 8), 0) % 8 == lax.broadcasted_iota(
        jnp.int32, (128, 8), 1
    )
    live = jnp.sum(jnp.where(picked, spread, 0.0), axis=1, keepdims=True)
    query = trip[:, :, 0:768].reshape(128, 768).astype(F32) * live
    qs[...] = query.astype(BF16).reshape(16, 8, 768)

    meet(everyone)

    def share(z, first):
        return (
            pl.ds(pl.multiple_of((z % 2) * 8, 8), 8),
            slice(None),
            pl.ds(pl.multiple_of(first + (z // 2) * 384, 128), 384),
        )

    kz = [links.copy(trip.at[share(z, 768)], kbuf.at[me.y, me.zl], dev) for z, dev in along_z]
    qz = [links.copy(qs.at[share(z, 0)], qbuf.at[me.zl], dev) for z, dev in along_z]
    vz = [links.copy(trip.at[share(z, 1536)], vbuf.at[me.y, me.zl], dev) for z, dev in along_z]
    kbuf[me.y, me.zl] = trip[share(me.zl, 768)]
    vbuf[me.y, me.zl] = trip[share(me.zl, 1536)]
    qbuf[me.zl] = qs[share(me.zl, 0)]

    def around_y(buf, arrivals):
        ups, downs = [], []
        for d in range(4):
            if d > 0:
                arrivals[d - 1].wait_recv()
            z = (me.zl + 4 - d) % 4
            piece = buf.at[me.y, z]
            ups.append(links.copy(piece, piece, up))
            downs.append(links.copy(piece, piece, down))
        return ups, downs

    def relay_y(buf, ups, downs):
        more = []
        for d in range(2):
            ups[d].wait_recv()
            z = (me.zl + 4 - d) % 4
            piece = buf.at[y_down, z]
            more.append(links.copy(piece, piece, up))
            downs[d + 2].wait_recv()
            z = (me.zl + 4 - d - 2) % 4
            piece = buf.at[y_up, z]
            more.append(links.copy(piece, piece, down))
        return ups[2:] + downs[:2] + more

    kups, kdowns = around_y(kbuf, kz)
    rest = relay_y(kbuf, kups, kdowns)
    for q in qz:
        q.wait_recv()
    for k in rest:
        k.wait_recv()

    low = lax.broadcasted_iota(jnp.int32, (1, 128), 1) < 64
    low_b, high_b = low.astype(F32).astype(BF16), 1.0 - low.astype(F32)
    high_b = high_b.astype(BF16)

    def add_logits(r, totals):
        q = qbuf[:, r].reshape(32, 384)
        k = kbuf[:, :, r].reshape(128, 384)
        new = []
        for p in range(3):
            mine = q[:, 128 * p : 128 * p + 128]
            both = jnp.concatenate([mine * low_b, mine * high_b], axis=0)
            new.append(
                totals[p]
                + lax.dot_general(
                    both,
                    k[:, 128 * p : 128 * p + 128],
                    (((1,), (1,)), ((), ())),
                    preferred_element_type=F32,
                )
            )
        return tuple(new)

    totals = lax.fori_loop(0, 8, add_logits, (jnp.zeros((64, 128), F32),) * 3)
    scale = 1.0 / (math.sqrt(DH) * math.sqrt(512))
    logits = jnp.concatenate(totals, axis=0) * scale
    for g in range(8):
        lsend[g] = logits[24 * g : 24 * g + 24]
    parts = []
    for d in range(1, 8):
        g, dev = me.in_group(d)
        parts.append(links.copy(lsend.at[g], lrecv.at[me.group()], dev))
    lrecv[me.group()] = lsend[me.group()]
    vups, vdowns = around_y(vbuf, vz)
    for part in parts:
        part.wait_recv()
    total = lrecv[0]
    for g in range(1, 8):
        total = total + lrecv[g]
    erecv[me.cousin()] = total
    parts = []
    for d in range(1, 8):
        _, dev = me.in_cousins(d)
        slot = erecv.at[me.cousin()]
        parts.append(links.copy(slot, slot, dev))
    vrest = relay_y(vbuf, vups, vdowns)
    for part in parts:
        part.wait_recv()
    total = erecv[0]
    for e in range(1, 8):
        total = total + erecv[e]
    top = jnp.max(total, axis=1, keepdims=True)
    grown = jnp.exp(total - top)
    probs = (grown / jnp.sum(grown, axis=1, keepdims=True)).astype(BF16)
    pbuf[me.group()] = probs
    parts = []
    for d in range(1, 8):
        _, dev = me.in_group(d)
        slot = pbuf.at[me.group()]
        parts.append(links.copy(slot, slot, dev))
    for part in vrest + parts:
        part.wait_recv()
    all_probs = pbuf[...].reshape(192, 128)

    def context(r, carry):
        v = vbuf[:, :, r].reshape(128, 384)
        made = []
        for p in range(3):
            both = jnp.dot(
                all_probs[64 * p : 64 * p + 64],
                v[:, 128 * p : 128 * p + 128],
                preferred_element_type=F32,
            )
            made.append(jnp.where(low, both[:32], both[32:]))
        csend[:, r] = jnp.concatenate(made, axis=1).astype(BF16).reshape(4, 8, 384)
        return carry

    lax.fori_loop(0, 8, context, 0)
    back = [links.copy(csend.at[z], crecv.at[me.zl], dev) for z, dev in along_z]
    crecv[me.zl] = csend[me.zl]
    for b in back:
        b.wait_recv()
    out[...] = crecv[...]
    links.finish()


def row_attention(trip, occ):
    vmem = pl.BlockSpec(memory_space=pltpu.VMEM)
    n = 9 + 24 + 21 + 3
    return pl.pallas_call(
        row_kernel,
        out_shape=jax.ShapeDtypeStruct((4, 8, 8, 384), BF16),
        in_specs=[vmem, vmem],
        out_specs=vmem,
        scratch_shapes=[
            pltpu.VMEM((16, 8, 768), BF16),
            pltpu.VMEM((4, 4, 8, 8, 384), BF16),
            pltpu.VMEM((4, 4, 8, 8, 384), BF16),
            pltpu.VMEM((4, 8, 8, 384), BF16),
            pltpu.VMEM((8, 24, 128), F32),
            pltpu.VMEM((8, 24, 128), F32),
            pltpu.VMEM((8, 24, 128), F32),
            pltpu.VMEM((8, 24, 128), BF16),
            pltpu.VMEM((4, 8, 8, 384), BF16),
            pltpu.VMEM((4, 8, 8, 384), BF16),
            pltpu.SemaphoreType.DMA((n,)),
            pltpu.SemaphoreType.DMA((n,)),
        ],
        compiler_params=pltpu.CompilerParams(
            collective_id=1, has_side_effects=True, vmem_limit_bytes=40 * 1024 * 1024
        ),
        cost_estimate=pl.CostEstimate(flops=400000000, bytes_accessed=4000000, transcendentals=3000),
        name="row_attention",
    )(trip, occ)


COL = ("col",)


def in_one_piece(arrays, axis, dim, along):
    ends, at = ([], 0)
    for a in arrays[:-1]:
        at += a.shape[along]
        ends.append(at)
    both = jnp.concatenate(arrays, axis=along)
    return tuple(jnp.split(lax.all_gather(both, axis, axis=dim, tiled=True), ends, axis=along))


def from_everyone(array, axis):
    length = lax.axis_size(axis)
    return lax.all_to_all(
        jnp.broadcast_to(array[None], (length, *array.shape)), axis, 0, 0, tiled=True
    )


def of_everyone(array, axis):
    return from_everyone(array, axis).sum(axis=0)


def whole_of(array, axes, dim):
    filled = array
    for number in range(len(axes) - 1, -1, -1):
        filled = lax.all_gather(filled, axes[number], axis=dim, tiled=True)
    return filled


def items_in_groups(array, axis, split_dim, concat_dim, work, item_dim, out_dim):
    items = jax.tree.leaves(array)[0].shape[item_dim]
    count = 2 if items % 2 == 0 else 1
    gathered = []
    for k in range(count):
        group = jax.tree.map(
            lambda a: lax.slice_in_dim(
                a, k * (items // count), (k + 1) * (items // count), axis=item_dim
            ),
            array,
        )
        gathered.append(
            work(
                lax.all_to_all(
                    group, axis, split_axis=split_dim, concat_axis=concat_dim, tiled=True
                )
            )
        )
    return jax.tree.map(lambda *parts: jnp.concatenate(parts, axis=out_dim), *gathered)


def attend_columns(pieces):
    block, keep = pieces
    cq = block[..., :DH]
    ck = block[..., DH : 2 * DH]
    cv = block[..., 2 * DH :]
    scores = jnp.einsum("rgud,sgud->gurs", cq, ck, preferred_element_type=jnp.float32) / math.sqrt(
        DH
    )
    mask_keys = jnp.transpose(keep, (1, 2, 0))[:, :, None, :]
    scores = jnp.where(mask_keys > 0, scores, -1000000000.0)
    probs = jax.nn.softmax(scores, axis=-1).astype(jnp.bfloat16)
    return jnp.einsum("gurs,sgud->rgud", probs, cv, preferred_element_type=jnp.float32).astype(
        jnp.bfloat16
    )


def per_device(
    alignment_embedding_tensor,
    horizontal_attention_triples,
    occupancy_indicator,
    horizontal_attention_exit_matrix,
    vertical_attention_entry_matrix,
    vertical_attention_exit_matrix,
    vertical_layernorm_scaling,
):
    protein_extent, site_extent, embedding_dimension = alignment_embedding_tensor.shape
    live = occupancy_indicator.astype(jnp.bfloat16)
    full_wo_row, full_qkv, full_wo_col = in_one_piece(
        (
            horizontal_attention_exit_matrix,
            vertical_attention_entry_matrix,
            vertical_attention_exit_matrix,
        ),
        COL,
        0,
        1,
    )
    context = row_attention(horizontal_attention_triples, occupancy_indicator)
    merged_attended_heads = jnp.transpose(
        context.reshape(2, protein_extent * site_extent, 384), (1, 0, 2)
    ).reshape(protein_extent * site_extent, embedding_dimension)
    skip_connection_hidden = alignment_embedding_tensor.reshape(
        protein_extent * site_extent, embedding_dimension
    ).astype(jnp.float32) + jnp.dot(
        merged_attended_heads, full_wo_row, preferred_element_type=jnp.float32
    )
    center = skip_connection_hidden - jnp.mean(skip_connection_hidden, axis=-1, keepdims=True)
    variance = jnp.mean(center * center, axis=-1, keepdims=True)
    normed = (center * lax.rsqrt(variance + 1e-05) * vertical_layernorm_scaling).astype(
        jnp.bfloat16
    )
    col_qkv = jnp.dot(normed, full_qkv, preferred_element_type=jnp.float32).astype(jnp.bfloat16)
    seq_count = lax.axis_size("seq")
    units = site_extent * H // seq_count
    col_qkv = jnp.transpose(col_qkv.reshape(protein_extent, site_extent, 3, H, DH), (0, 1, 3, 2, 4))
    col_qkv = col_qkv.reshape(protein_extent, seq_count, units, 3 * DH)
    live_units = jnp.broadcast_to(live[:, :, None], (protein_extent, site_extent, H)).reshape(
        protein_extent, seq_count, units
    )
    attended = items_in_groups((col_qkv, live_units), "seq", 1, 0, attend_columns, 2, 2)
    returned_cols = lax.all_to_all(attended, "seq", split_axis=0, concat_axis=1, tiled=True)
    col_context = returned_cols.reshape(protein_extent * site_extent, embedding_dimension)
    mixed = skip_connection_hidden + jnp.dot(
        col_context, full_wo_col, preferred_element_type=jnp.float32
    )
    return mixed.reshape(protein_extent, site_extent, embedding_dimension)


def solution(mesh):
    in_specs = (
        P("seq", COL, None),
        P("seq", COL, None),
        P("seq", COL),
        P(COL, None),
        P(COL, None),
        P(COL, None),
        P(),
    )
    out_specs = P("seq", COL, None)
    return jax.shard_map(
        per_device, mesh=mesh, in_specs=in_specs, out_specs=out_specs, check_vma=False
    )
```

```python
import functools
import math

import jax
import jax.numpy as jnp
from jax import lax
from jax.experimental import pallas as pl
from jax.experimental.pallas import tpu as pltpu
from jax.sharding import Mesh
from jax.sharding import PartitionSpec as P

H = 12
DH = 64
F32 = jnp.float32
BF16 = jnp.bfloat16
MESH = pl.DeviceIdType.MESH


class Links:
    def __init__(self, send_sem, recv_sem):
        self.send_sem, self.recv_sem, self.count, self.started = send_sem, recv_sem, 0, []

    def copy(self, src, dst, device):
        k = self.count
        self.count += 1
        made = pltpu.make_async_remote_copy(
            src_ref=src,
            dst_ref=dst,
            send_sem=self.send_sem.at[k],
            recv_sem=self.recv_sem.at[k],
            device_id=device,
            device_id_type=MESH,
        )
        made.start()
        self.started.append(made)
        return made

    def finish(self):
        for made in self.started:
            made.wait_send()


class Place:
    def __init__(self):
        s, c = lax.axis_index("seq"), lax.axis_index("col")
        self.x, self.zh, self.co = s // 8, (s // 2) % 4, s % 2
        self.y, self.zl = c // 4, c % 4

    def at(self, **moved):
        g = {k: moved.get(k, getattr(self, k)) for k in ("x", "zh", "co", "y", "zl")}
        return (g["x"] * 8 + g["zh"] * 2 + g["co"], g["y"] * 4 + g["zl"])

    def group(self):
        return self.x * 2 + self.co

    def in_group(self, d):
        g = (self.group() + d) % 8
        return g, self.at(x=g // 2, co=g % 2)

    def cousin(self):
        return self.zh * 2 + self.zl % 2

    def on_ring(self, d):
        z = (4 * self.zh + self.zl + d + 16) % 16
        return self.at(zh=z // 4, zl=z % 4)

    def in_cousins(self, d):
        e = (self.cousin() + d) % 8
        return e, self.at(zh=e // 2, zl=(self.zl // 2) * 2 + e % 2)


def meet(devices):
    barrier = pltpu.get_barrier_semaphore()
    for device in devices:
        pl.semaphore_signal(barrier, inc=1, device_id=device, device_id_type=MESH)
    pl.semaphore_wait(barrier, len(devices))


class Weights:
    def __init__(self, me, links, buf, up, down):
        self.me, self.links, self.buf, self.up, self.down = me, links, buf, up, down
        self.half = pl.ds(3 * (me.x % 2), 3)
        self.y_up, self.y_down, self.y_far = (me.y + 1) % 4, (me.y + 3) % 4, (me.y + 2) % 4

    def over_z(self):
        piece = self.buf.at[self.me.y, self.me.zl, self.half]
        self.z = [self.links.copy(piece, piece, self.me.on_ring(d)) for d in (1, -1, 2)]

    def over_y(self):
        for z in self.z:
            z.wait_recv()
        piece = self.buf.at[self.me.y, :, self.half]
        self.ups = self.links.copy(piece, piece, self.up)
        self.downs = self.links.copy(piece, piece, self.down)
        self.right, self.left = self.me.at(x=(self.me.x + 1) % 4), self.me.at(x=(self.me.x + 3) % 4)
        self.xs = [self.links.copy(piece, piece, self.right)]

    def relay_y(self):
        self.ups.wait_recv()
        piece = self.buf.at[self.y_down, 0:2, self.half]
        self.far = [self.links.copy(piece, piece, self.up)]
        self.downs.wait_recv()
        piece = self.buf.at[self.y_up, 2:4, self.half]
        self.far.append(self.links.copy(piece, piece, self.down))
        piece = self.buf.at[self.y_up, :, self.half]
        self.xs.append(self.links.copy(piece, piece, self.right))
        piece = self.buf.at[self.y_down, :, self.half]
        self.xs.append(self.links.copy(piece, piece, self.left))

    def over_x(self):
        for f in self.far:
            f.wait_recv()
        piece = self.buf.at[self.y_far, :, self.half]
        self.xs.append(self.links.copy(piece, piece, self.left))

    def arrive(self):
        for x in self.xs:
            x.wait_recv()


def layer_kernel(
    emb, trip, occ, wr, wq, wc, gain, out,
    qs, kbuf, vbuf, qbuf, lsend, lrecv, erecv, pbuf, csend, crecv,
    wobuf, wqbuf, mslot, mx, resid, nsend, fbuf, nb, kc, vc, qc, asend, arecv,
    send_sem, recv_sem,
):
    me = Place()
    links = Links(send_sem, recv_sem)
    along_z = [((me.zl + d) % 4, me.at(zl=(me.zl + d) % 4)) for d in range(1, 4)]
    y_up, y_down = (me.y + 1) % 4, (me.y + 3) % 4
    up, down = me.at(y=y_up), me.at(y=y_down)
    everyone = [d for _, d in along_z] + [up, down] + [me.in_group(d)[1] for d in range(1, 8)]
    everyone += [me.on_ring(d) for d in (1, -1, 2, -2)]
    for d in range(1, 4):
        zh = (me.zh + d) % 4
        everyone.append(me.at(zh=zh, zl=(me.zl // 2) * 2 + (me.zl + 1) % 2))
        for co in range(2):
            everyone.append(me.at(zh=zh, co=(me.co + co) % 2))
            everyone.append(me.at(zh=zh, co=(me.co + co) % 2, x=3 - me.x))

    rows = lax.broadcasted_iota(jnp.int32, (128, 16), 0)
    seqs = lax.broadcasted_iota(jnp.int32, (128, 16), 1)
    spread = jnp.dot(
        (rows // 8 == seqs).astype(BF16), occ[...].astype(F32).astype(BF16), preferred_element_type=F32
    )
    picked = lax.broadcasted_iota(jnp.int32, (128, 8), 0) % 8 == lax.broadcasted_iota(
        jnp.int32, (128, 8), 1
    )
    live = jnp.sum(jnp.where(picked, spread, 0.0), axis=1, keepdims=True)
    query = trip[:, :, 0:768].reshape(128, 768).astype(F32) * live
    qs[...] = query.astype(BF16).reshape(16, 8, 768)

    lane = lax.broadcasted_iota(jnp.int32, (16, 128), 1)
    mine = (lane % 16 == lax.broadcasted_iota(jnp.int32, (16, 128), 0)) & (
        lane // 16 == me.co * 4 + me.zh
    )
    mslot[me.zh * 2 + me.co] = lax.dot_general(
        occ[...].astype(F32).astype(BF16),
        mine.astype(F32).astype(BF16),
        (((0,), (0,)), ((), ())),
        preferred_element_type=F32,
    )
    w_o = Weights(me, links, wobuf.at[me.co], up, down)
    w_q = Weights(me, links, wqbuf, up, down)
    first = (me.co == 0).astype(F32)
    both_o = wr[w_o.half].astype(F32) * first + wc[w_o.half].astype(F32) * (1.0 - first)
    wobuf[me.co, me.y, me.zl, w_o.half] = both_o.astype(BF16)
    for t in range(3):
        at = pl.ds(pl.multiple_of(768 * t + 384 * me.co, 128), 384)
        wqbuf[me.y, me.zl, w_q.half, :, 384 * t : 384 * t + 384] = wq[w_q.half, :, at]

    meet(everyone)

    def share(z, first):
        return (
            pl.ds(pl.multiple_of((z % 2) * 8, 8), 8),
            slice(None),
            pl.ds(pl.multiple_of(first + (z // 2) * 384, 128), 384),
        )

    kz = [links.copy(trip.at[share(z, 768)], kbuf.at[me.y, me.zl], dev) for z, dev in along_z]
    w_o.over_z()
    qz = [links.copy(qs.at[share(z, 0)], qbuf.at[me.zl], dev) for z, dev in along_z]
    vz = [links.copy(trip.at[share(z, 1536)], vbuf.at[me.y, me.zl], dev) for z, dev in along_z]
    w_q.over_z()
    marks = []
    slot = mslot.at[me.zh * 2 + me.co]
    for d in range(1, 8):
        e = (me.zh * 2 + me.co + d) % 8
        marks.append(links.copy(slot, slot, me.at(zh=e // 2, co=e % 2)))
    kbuf[me.y, me.zl] = trip[share(me.zl, 768)]
    vbuf[me.y, me.zl] = trip[share(me.zl, 1536)]
    qbuf[me.zl] = qs[share(me.zl, 0)]

    def around_y(buf, arrivals):
        ups, downs = [], []
        for d in range(4):
            if d > 0:
                arrivals[d - 1].wait_recv()
            z = (me.zl + 4 - d) % 4
            piece = buf.at[me.y, z]
            ups.append(links.copy(piece, piece, up))
            downs.append(links.copy(piece, piece, down))
        return ups, downs

    def relay_y(buf, ups, downs):
        more = []
        for d in range(2):
            ups[d].wait_recv()
            z = (me.zl + 4 - d) % 4
            piece = buf.at[y_down, z]
            more.append(links.copy(piece, piece, up))
            downs[d + 2].wait_recv()
            z = (me.zl + 4 - d - 2) % 4
            piece = buf.at[y_up, z]
            more.append(links.copy(piece, piece, down))
        return ups[2:] + downs[:2] + more

    kups, kdowns = around_y(kbuf, kz)
    w_o.over_y()
    rest = relay_y(kbuf, kups, kdowns)
    for mark in marks:
        mark.wait_recv()
    marked = mslot[0]
    for e in range(1, 8):
        marked = marked + mslot[e]
    mx[me.x] = marked
    marks = []
    for d in range(1, 4):
        marks.append(links.copy(mx.at[me.x], mx.at[me.x], me.at(x=(me.x + d) % 4)))
    w_o.relay_y()
    for q in qz:
        q.wait_recv()
    for k in rest:
        k.wait_recv()

    low = lax.broadcasted_iota(jnp.int32, (1, 128), 1) < 64
    low_b, high_b = low.astype(F32).astype(BF16), 1.0 - low.astype(F32)
    high_b = high_b.astype(BF16)

    def add_logits(r, totals):
        q = qbuf[:, r].reshape(32, 384)
        k = kbuf[:, :, r].reshape(128, 384)
        new = []
        for p in range(3):
            mine = q[:, 128 * p : 128 * p + 128]
            both = jnp.concatenate([mine * low_b, mine * high_b], axis=0)
            new.append(
                totals[p]
                + lax.dot_general(
                    both,
                    k[:, 128 * p : 128 * p + 128],
                    (((1,), (1,)), ((), ())),
                    preferred_element_type=F32,
                )
            )
        return tuple(new)

    totals = lax.fori_loop(0, 8, add_logits, (jnp.zeros((64, 128), F32),) * 3)
    scale = 1.0 / (math.sqrt(DH) * math.sqrt(512))
    logits = jnp.concatenate(totals, axis=0) * scale
    for g in range(8):
        lsend[g] = logits[24 * g : 24 * g + 24]
    parts = []
    for d in range(1, 8):
        g, dev = me.in_group(d)
        parts.append(links.copy(lsend.at[g], lrecv.at[me.group()], dev))
    lrecv[me.group()] = lsend[me.group()]
    vups, vdowns = around_y(vbuf, vz)
    w_o.over_x()
    for part in parts:
        part.wait_recv()
    total = lrecv[0]
    for g in range(1, 8):
        total = total + lrecv[g]
    erecv[me.cousin()] = total
    parts = []
    for d in range(1, 8):
        _, dev = me.in_cousins(d)
        slot = erecv.at[me.cousin()]
        parts.append(links.copy(slot, slot, dev))
    vrest = relay_y(vbuf, vups, vdowns)
    w_q.over_y()
    for part in parts:
        part.wait_recv()
    total = erecv[0]
    for e in range(1, 8):
        total = total + erecv[e]
    top = jnp.max(total, axis=1, keepdims=True)
    grown = jnp.exp(total - top)
    probs = (grown / jnp.sum(grown, axis=1, keepdims=True)).astype(BF16)
    pbuf[me.group()] = probs
    parts = []
    for d in range(1, 8):
        _, dev = me.in_group(d)
        slot = pbuf.at[me.group()]
        parts.append(links.copy(slot, slot, dev))
    core = me.at(co=1 - me.co)
    piece = wobuf.at[me.co, :, :, w_o.half]
    w_cores = [links.copy(piece, piece, core)]
    w_o.arrive()
    piece = wobuf.at[me.co, :, :, pl.ds(3 - 3 * (me.x % 2), 3)]
    w_cores.append(links.copy(piece, piece, core))
    w_q.relay_y()
    for part in vrest + parts:
        part.wait_recv()
    all_probs = pbuf[...].reshape(192, 128)

    def context(r, carry):
        v = vbuf[:, :, r].reshape(128, 384)
        made = []
        for p in range(3):
            both = jnp.dot(
                all_probs[64 * p : 64 * p + 64],
                v[:, 128 * p : 128 * p + 128],
                preferred_element_type=F32,
            )
            made.append(jnp.where(low, both[:32], both[32:]))
        csend[:, r] = jnp.concatenate(made, axis=1).astype(BF16).reshape(4, 8, 384)
        return carry

    lax.fori_loop(0, 8, context, 0)
    back = [links.copy(csend.at[z], crecv.at[me.zl], dev) for z, dev in along_z]
    crecv[me.zl] = csend[me.zl]
    for b in back:
        b.wait_recv()
    w_q.over_x()
    for w in w_cores:
        w.wait_recv()

    w_row = wobuf[0].reshape(768, 768)
    mixed = emb[...].reshape(128, 768).astype(F32)
    for h in range(2):
        mixed = mixed + jnp.dot(
            crecv[2 * h : 2 * h + 2].reshape(128, 384),
            w_row[384 * h : 384 * h + 384],
            preferred_element_type=F32,
        )
    resid[...] = mixed
    center = mixed - jnp.mean(mixed, axis=-1, keepdims=True)
    variance = jnp.mean(center * center, axis=-1, keepdims=True)
    normed = (center * lax.rsqrt(variance + 1e-05) * gain[...]).astype(BF16)
    above = lax.broadcasted_iota(jnp.int32, (128, 128), 0)
    along = lax.broadcasted_iota(jnp.int32, (128, 128), 1)
    turn = (along == (above % 16) * 8 + above // 16).astype(F32).astype(BF16)
    turned = jnp.dot(turn, normed, preferred_element_type=F32).astype(BF16)
    nsend[...] = turned.reshape(8, 16, 768)

    pair = me.x // 2
    step1 = {}
    for d in (2, 1, 3):
        zh = (me.zh + d) % 4
        dev = me.at(zh=zh)
        step1[d] = (
            links.copy(nsend.at[2 * zh + pair], nb.at[me.x, me.co, me.zh], dev),
            links.copy(nsend.at[2 * zh + 1 - pair], fbuf.at[me.zh], dev),
        )
    nb[me.x, me.co, me.zh] = nsend[2 * me.zh + pair]
    fbuf[me.zh] = nsend[2 * me.zh + 1 - pair]
    x_mate = (me.x // 2) * 2 + 1 - me.x % 2
    x_over = 3 - me.x
    mate, over = me.at(x=x_mate), me.at(x=x_over)
    to_mate, to_over, to_core, onward = {}, {}, [], []

    def on_arrival(d):
        if d > 0:
            for made in step1[d]:
                made.wait_recv()
        z = (me.zh + 4 - d) % 4
        piece = nb.at[me.x, me.co, z]
        to_over[d] = links.copy(fbuf.at[z], piece, over)
        to_mate[d] = links.copy(piece, piece, mate)
        to_core.append(links.copy(piece, piece, core))

    def pass_on(d):
        z = (me.zh + 4 - d) % 4
        to_over[d].wait_recv()
        piece = nb.at[x_over, me.co, z]
        onward.append(links.copy(piece, piece, mate))
        to_core.append(links.copy(piece, piece, core))
        to_mate[d].wait_recv()
        piece = nb.at[x_mate, me.co, z]
        to_core.append(links.copy(piece, piece, core))

    order = (0, 1, 3, 2)
    for n, d in enumerate(order):
        on_arrival(d)
        if n > 0:
            pass_on(order[n - 1])
    pass_on(order[-1])
    for n, d in enumerate(order):
        z = (me.zh + 4 - d) % 4
        onward[n].wait_recv()
        piece = nb.at[3 - x_mate, me.co, z]
        to_core.append(links.copy(piece, piece, core))
    w_q.arrive()
    for made in marks + to_core:
        made.wait_recv()

    tokens = nb[...].reshape(512, 768)
    w_kv = wqbuf[:, :, :, :, 384:1152].reshape(768, 768)
    keys_values = jnp.dot(tokens, w_kv, preferred_element_type=F32).astype(BF16)
    for p in range(3):
        kc[p] = keys_values[:, 128 * p : 128 * p + 128]
        vc[p] = keys_values[:, 384 + 128 * p : 512 + 128 * p]
    asking = jnp.concatenate([nb[me.x].reshape(128, 768), nb[x_over].reshape(128, 768)], axis=0)
    w_queries = wqbuf[:, :, :, :, 0:384].reshape(768, 384)
    queries = jnp.dot(asking, w_queries, preferred_element_type=F32).astype(BF16)
    for p in range(3):
        qc[p] = queries[:, 128 * p : 128 * p + 128]

    everywhere = jnp.concatenate([mx[x] for x in range(4)], axis=1)
    column = lax.broadcasted_iota(jnp.int32, (8, 512), 0) == 2 * me.zh + pair
    keep = jnp.sum(jnp.where(column, everywhere, 0.0), axis=0, keepdims=True) > 0

    def attend(p, carry):
        k, v = kc[p], vc[p]
        for b in range(4):
            q = qc[p, 64 * b : 64 * b + 64]
            both = jnp.concatenate([q * low_b, q * high_b], axis=0)
            scores = lax.dot_general(
                both, k, (((1,), (1,)), ((), ())), preferred_element_type=F32
            ) * (1.0 / math.sqrt(DH))
            scores = jnp.where(keep, scores, -1000000000.0)
            grown = jnp.exp(scores - jnp.max(scores, axis=1, keepdims=True))
            size = jnp.sum(grown, axis=1, keepdims=True)
            made = jnp.dot(grown.astype(BF16), v, preferred_element_type=F32) / size
            made = jnp.where(low, made[:64], made[64:]).astype(BF16)
            asend[b // 2, b % 2, p] = made.reshape(4, 16, 128)
        return carry

    lax.fori_loop(0, 3, attend, 0)

    mine = 2 * me.zh + pair
    backs = []
    for d in (2, 1, 3, 0):
        zh = (me.zh + d) % 4
        for far in range(2):
            for other in range(2):
                if d == far == other == 0:
                    continue
                co = (me.co + other) % 2
                x = x_over if far else me.x
                backs.append(
                    links.copy(
                        asend.at[far, co, :, zh], arecv.at[mine, me.co], me.at(x=x, zh=zh, co=co)
                    )
                )
    arecv[mine, me.co] = asend[0, me.co, :, me.zh]
    for made in backs:
        made.wait_recv()
    w_col = wobuf[1].reshape(768, 768)
    turn_back = (above == (along % 16) * 8 + along // 16).astype(F32).astype(BF16)
    attended = jnp.concatenate(
        [arecv[:, h, p].reshape(128, 128) for h in range(2) for p in range(3)], axis=1
    )
    attended = jnp.dot(turn_back, attended, preferred_element_type=F32).astype(BF16)
    out[...] = resid[...] + jnp.dot(attended, w_col, preferred_element_type=F32)
    links.finish()


def per_device(emb, trip, occ, wr, wq, wc, gain):
    vmem = pl.BlockSpec(memory_space=pltpu.VMEM)
    n = 160
    out = pl.pallas_call(
        layer_kernel,
        out_shape=jax.ShapeDtypeStruct((128, 768), F32),
        in_specs=[vmem] * 7,
        out_specs=vmem,
        scratch_shapes=[
            pltpu.VMEM((16, 8, 768), BF16),
            pltpu.VMEM((4, 4, 8, 8, 384), BF16),
            pltpu.VMEM((4, 4, 8, 8, 384), BF16),
            pltpu.VMEM((4, 8, 8, 384), BF16),
            pltpu.VMEM((8, 24, 128), F32),
            pltpu.VMEM((8, 24, 128), F32),
            pltpu.VMEM((8, 24, 128), F32),
            pltpu.VMEM((8, 24, 128), BF16),
            pltpu.VMEM((4, 8, 8, 384), BF16),
            pltpu.VMEM((4, 8, 8, 384), BF16),
            pltpu.VMEM((2, 4, 4, 6, 8, 768), BF16),
            pltpu.VMEM((4, 4, 6, 8, 1152), BF16),
            pltpu.VMEM((8, 8, 128), F32),
            pltpu.VMEM((4, 8, 128), F32),
            pltpu.VMEM((128, 768), F32),
            pltpu.VMEM((8, 16, 768), BF16),
            pltpu.VMEM((4, 16, 768), BF16),
            pltpu.VMEM((4, 2, 4, 16, 768), BF16),
            pltpu.VMEM((3, 512, 128), BF16),
            pltpu.VMEM((3, 512, 128), BF16),
            pltpu.VMEM((3, 256, 128), BF16),
            pltpu.VMEM((2, 2, 3, 4, 16, 128), BF16),
            pltpu.VMEM((8, 2, 3, 16, 128), BF16),
            pltpu.SemaphoreType.DMA((n,)),
            pltpu.SemaphoreType.DMA((n,)),
        ],
        compiler_params=pltpu.CompilerParams(
            collective_id=1, has_side_effects=True, vmem_limit_bytes=48 * 1024 * 1024
        ),
        name="msa_layer",
    )(
        emb,
        trip,
        occ,
        wr.reshape(6, 8, 768),
        wq.reshape(6, 8, 2304),
        wc.reshape(6, 8, 768),
        gain.reshape(1, 768),
    )
    return out.reshape(16, 8, 768)


def solution(mesh):
    both = P("seq", "col", None)
    return jax.shard_map(
        per_device,
        mesh=mesh,
        in_specs=(both, both, P("seq", "col"), P("col", None), P("col", None), P("col", None), P()),
        out_specs=both,
        check_vma=False,
    )
```

```python
import functools
import math

import jax
import jax.numpy as jnp
from jax import lax
from jax.experimental import pallas as pl
from jax.experimental.pallas import tpu as pltpu
from jax.sharding import Mesh
from jax.sharding import PartitionSpec as P

H = 12
DH = 64
F32 = jnp.float32
BF16 = jnp.bfloat16
MESH = pl.DeviceIdType.MESH


class Links:
    def __init__(self, send_sem, recv_sem):
        self.send_sem, self.recv_sem, self.count, self.started = send_sem, recv_sem, 0, []

    def copy(self, src, dst, device):
        k = self.count
        self.count += 1
        made = pltpu.make_async_remote_copy(
            src_ref=src,
            dst_ref=dst,
            send_sem=self.send_sem.at[k],
            recv_sem=self.recv_sem.at[k],
            device_id=device,
            device_id_type=MESH,
        )
        made.start()
        self.started.append(made)
        return made

    def finish(self):
        for made in self.started:
            made.wait_send()


class Place:
    def __init__(self):
        s, c = lax.axis_index("seq"), lax.axis_index("col")
        self.x, self.zh, self.co = s // 8, (s // 2) % 4, s % 2
        self.y, self.zl = c // 4, c % 4

    def at(self, **moved):
        g = {k: moved.get(k, getattr(self, k)) for k in ("x", "zh", "co", "y", "zl")}
        return (g["x"] * 8 + g["zh"] * 2 + g["co"], g["y"] * 4 + g["zl"])

    def group(self):
        return self.x * 4 + self.co * 2 + self.zl % 2

    def in_group(self, d):
        g = (self.group() + d) % 16
        return g, self.at(x=g // 4, co=(g // 2) % 2, zl=(self.zl // 2) * 2 + g % 2)

    def on_ring(self, d):
        z = (4 * self.zh + self.zl + d + 16) % 16
        return self.at(zh=z // 4, zl=z % 4)


def meet(devices):
    barrier = pltpu.get_barrier_semaphore()
    for device in devices:
        pl.semaphore_signal(barrier, inc=1, device_id=device, device_id_type=MESH)
    pl.semaphore_wait(barrier, len(devices))


class Weights:
    def __init__(self, me, links, buf, rows, up, down):
        self.me, self.links, self.buf, self.rows, self.up, self.down = me, links, buf, rows, up, down
        self.y_up, self.y_down, self.y_far = (me.y + 1) % 4, (me.y + 3) % 4, (me.y + 2) % 4
        self.right, self.left = me.at(x=(me.x + 1) % 4), me.at(x=(me.x + 3) % 4)
        self.xs = []

    def send(self, piece, device):
        return self.links.copy(piece, piece, device)

    def over_z(self):
        piece = self.buf.at[self.me.y, self.me.zl, self.rows]
        self.z = [self.send(piece, self.me.on_ring(d)) for d in (1, -1, 2)]

    def over_y(self):
        for z in self.z:
            z.wait_recv()
        piece = self.buf.at[self.me.y, :, self.rows]
        self.ups = self.send(piece, self.up)
        self.downs = self.send(piece, self.down)

    def relay_y(self):
        self.ups.wait_recv()
        self.far = [self.send(self.buf.at[self.y_down, 0:2, self.rows], self.up)]
        self.downs.wait_recv()
        self.far.append(self.send(self.buf.at[self.y_up, 2:4, self.rows], self.down))

    def near_x(self):
        for y, device in ((self.me.y, self.right), (self.y_up, self.right), (self.y_down, self.left)):
            self.xs.append(self.send(self.buf.at[y, :, self.rows], device))

    def far_y(self):
        for f in self.far:
            f.wait_recv()

    def far_x(self):
        self.xs.append(self.send(self.buf.at[self.y_far, :, self.rows], self.left))

    def arrive(self):
        for x in self.xs:
            x.wait_recv()

    def to_core(self, core, rows):
        return self.send(self.buf.at[:, :, rows], core)


def layer_kernel(
    emb, trip, occ, wr, wq, wc, gain, out,
    qraw, qs, kbuf, vbuf, qbuf, lsend, lrecv, erecv, pbuf, csend, crecv,
    wrbuf, wcbuf, wqbuf, mslot, mx, resid, nsend, xr, nb, kc, vc, qc, asend, arecv,
    occ_in, emb_in, gain_in, send_sem, recv_sem, load_sem,
):
    me = Place()
    links = Links(send_sem, recv_sem)
    along_z = [((me.zl + d) % 4, me.at(zl=(me.zl + d) % 4)) for d in range(1, 4)]
    y_up, y_down = (me.y + 1) % 4, (me.y + 3) % 4
    up, down = me.at(y=y_up), me.at(y=y_down)
    everyone = [d for _, d in along_z] + [up, down] + [me.in_group(d)[1] for d in range(1, 16)]
    everyone += [me.on_ring(d) for d in (1, -1, 2, -2)]
    for d in range(1, 4):
        zh = (me.zh + d) % 4
        everyone.append(me.at(zh=zh, co=1 - me.co))
        for e in range(4):
            everyone.append(me.at(zh=zh, x=(me.x + e) % 4))

    loads = []

    def load(src, dst):
        made = pltpu.make_async_copy(src, dst, load_sem.at[len(loads)])
        made.start()
        loads.append(made)
        return made

    def share(z, first):
        return (
            pl.ds(pl.multiple_of((z % 2) * 8, 8), 8),
            slice(None),
            pl.ds(pl.multiple_of(first + (z // 2) * 384, 128), 384),
        )

    half, other_half = pl.ds(3 * (me.x % 2), 3), pl.ds(3 - 3 * (me.x % 2), 3)
    w_r = Weights(me, links, wrbuf.at[me.co], half, up, down)
    w_c = Weights(me, links, wcbuf.at[me.co], slice(None), up, down)
    core_half = pl.ds(3 * me.co, 3)
    w_q = Weights(me, links, wqbuf, core_half, up, down)
    core = me.at(co=1 - me.co)
    half_lanes = pl.ds(pl.multiple_of(384 * me.co, 128), 384)
    q_loads = [load(trip.at[:, :, 0:768], qraw), load(occ, occ_in)]
    k_load = load(trip.at[share(me.zl, 768)], kbuf.at[me.y, me.zl])
    w_loads = [
        load(wr.at[half, :, half_lanes], wrbuf.at[me.co, me.y, me.zl, half]),
        load(wc.at[:, :, half_lanes], wcbuf.at[me.co, me.y, me.zl]),
    ]
    for t in range(3):
        at = pl.ds(pl.multiple_of(768 * t + 384 * (me.x % 2), 128), 384)
        w_loads.append(
            load(
                wq.at[core_half, :, at],
                wqbuf.at[me.y, me.zl, core_half, :, 384 * t : 384 * t + 384],
            )
        )
    v_load = load(trip.at[share(me.zl, 1536)], vbuf.at[me.y, me.zl])
    last_loads = [load(emb, emb_in), load(gain, gain_in)]

    meet(everyone)

    kz = [links.copy(trip.at[share(z, 768)], kbuf.at[me.y, me.zl], dev) for z, dev in along_z]
    k_load.wait()
    piece = kbuf.at[me.y, me.zl]
    kups, kdowns = [links.copy(piece, piece, up)], [links.copy(piece, piece, down)]

    for made in q_loads:
        made.wait()
    rows = lax.broadcasted_iota(jnp.int32, (128, 16), 0)
    seqs = lax.broadcasted_iota(jnp.int32, (128, 16), 1)
    occupied = occ_in[...].astype(F32).astype(BF16)
    spread = lax.dot_general(
        (rows // 8 == seqs).astype(F32).astype(BF16),
        occupied,
        (((1,), (1,)), ((), ())),
        preferred_element_type=F32,
    )
    picked = lax.broadcasted_iota(jnp.int32, (128, 8), 0) % 8 == lax.broadcasted_iota(
        jnp.int32, (128, 8), 1
    )
    live = jnp.sum(jnp.where(picked, spread, 0.0), axis=1, keepdims=True)
    query = qraw[...].reshape(128, 768).astype(F32) * live
    qs[...] = query.astype(BF16).reshape(16, 8, 768)
    qz = [links.copy(qs.at[share(z, 0)], qbuf.at[me.zl], dev) for z, dev in along_z]
    for made in w_loads:
        made.wait()
    w_r.over_z()
    qbuf[me.zl] = qs[share(me.zl, 0)]

    lane = lax.broadcasted_iota(jnp.int32, (16, 128), 1)
    mine = (lane % 16 == lax.broadcasted_iota(jnp.int32, (16, 128), 0)) & (
        lane // 16 == me.co * 4 + me.zh
    )
    mslot[me.zh * 2 + me.co] = jnp.dot(
        occupied, mine.astype(F32).astype(BF16), preferred_element_type=F32
    )
    marks = []
    slot = mslot.at[me.zh * 2 + me.co]
    for d in range(1, 8):
        e = (me.zh * 2 + me.co + d) % 8
        marks.append(links.copy(slot, slot, me.at(zh=e // 2, co=e % 2)))

    def around_y(buf, arrivals, ups, downs):
        for d in range(len(ups), 4):
            if d > 0:
                arrivals[d - 1].wait_recv()
            piece = buf.at[me.y, (me.zl + 4 - d) % 4]
            ups.append(links.copy(piece, piece, up))
            downs.append(links.copy(piece, piece, down))

    def relay_y(buf, ups, downs):
        more = []
        for d in range(2):
            ups[d].wait_recv()
            z = (me.zl + 4 - d) % 4
            piece = buf.at[y_down, z]
            more.append(links.copy(piece, piece, up))
            downs[d + 2].wait_recv()
            z = (me.zl + 4 - d - 2) % 4
            piece = buf.at[y_up, z]
            more.append(links.copy(piece, piece, down))
        return ups[2:] + downs[:2] + more

    around_y(kbuf, kz, kups, kdowns)
    rest = relay_y(kbuf, kups, kdowns)
    w_r.over_y()
    for q in qz:
        q.wait_recv()
    vz = [links.copy(trip.at[share(z, 1536)], vbuf.at[me.y, me.zl], dev) for z, dev in along_z]
    for k in rest:
        k.wait_recv()

    low = lax.broadcasted_iota(jnp.int32, (1, 128), 1) < 64
    low_b, high_b = low.astype(F32).astype(BF16), 1.0 - low.astype(F32)
    high_b = high_b.astype(BF16)

    def add_logits(r, totals):
        q = qbuf[:, r].reshape(32, 384)
        k = kbuf[:, :, r].reshape(128, 384)
        new = []
        for p in range(3):
            mine = q[:, 128 * p : 128 * p + 128]
            both = jnp.concatenate([mine * low_b, mine * high_b], axis=0)
            new.append(
                totals[p]
                + lax.dot_general(
                    both,
                    k[:, 128 * p : 128 * p + 128],
                    (((1,), (1,)), ((), ())),
                    preferred_element_type=F32,
                )
            )
        return tuple(new)

    totals = lax.fori_loop(0, 8, add_logits, (jnp.zeros((64, 128), F32),) * 3)
    scale = 1.0 / (math.sqrt(DH) * math.sqrt(512))
    logits = jnp.concatenate(totals, axis=0) * scale
    for g in range(16):
        lsend[g] = logits[12 * g : 12 * g + 12]
    parts = []
    for d in range(1, 16):
        g, dev = me.in_group(d)
        parts.append(links.copy(lsend.at[g], lrecv.at[me.group()], dev))
    lrecv[me.group()] = lsend[me.group()]
    w_q.over_z()
    w_c.over_z()
    for part in parts:
        part.wait_recv()
    total = lrecv[0]
    for g in range(1, 16):
        total = total + lrecv[g]
    erecv[me.zh] = total
    parts = []
    for d in (2, 1, 3):
        slot = erecv.at[me.zh]
        parts.append(links.copy(slot, slot, me.at(zh=(me.zh + d) % 4)))
    v_load.wait()
    vups, vdowns = [], []
    around_y(vbuf, vz, vups, vdowns)
    w_r.relay_y()
    w_r.near_x()
    for part in parts:
        part.wait_recv()
    total = erecv[0]
    for e in range(1, 4):
        total = total + erecv[e]
    top = jnp.max(total, axis=1, keepdims=True)
    grown = jnp.exp(total - top)
    pbuf[me.group()] = grown / jnp.sum(grown, axis=1, keepdims=True)
    parts = []
    for d in range(1, 16):
        _, dev = me.in_group(d)
        slot = pbuf.at[me.group()]
        parts.append(links.copy(slot, slot, dev))
    vrest = relay_y(vbuf, vups, vdowns)
    w_r.far_y()
    w_r.far_x()
    w_cores = [w_r.to_core(core, half)]
    w_q.over_y()
    for mark in marks:
        mark.wait_recv()
    marked = mslot[0]
    for e in range(1, 8):
        marked = marked + mslot[e]
    mx[me.x] = marked
    marks = []
    for d in range(1, 4):
        marks.append(links.copy(mx.at[me.x], mx.at[me.x], me.at(x=(me.x + d) % 4)))
    for part in vrest + parts:
        part.wait_recv()
    all_probs = jnp.concatenate([pbuf[g] for g in range(16)], axis=0).astype(BF16)

    def context(r, carry):
        v = vbuf[:, :, r].reshape(128, 384)
        made = []
        for p in range(3):
            both = jnp.dot(
                all_probs[64 * p : 64 * p + 64],
                v[:, 128 * p : 128 * p + 128],
                preferred_element_type=F32,
            )
            made.append(jnp.where(low, both[:32], both[32:]))
        csend[:, r] = jnp.concatenate(made, axis=1).astype(BF16).reshape(4, 8, 384)
        return carry

    lax.fori_loop(0, 8, context, 0)
    back = [links.copy(csend.at[z], crecv.at[me.zl], dev) for z, dev in along_z]
    crecv[me.zl] = csend[me.zl]
    w_r.arrive()
    w_cores.append(w_r.to_core(core, other_half))
    w_q.relay_y()
    w_c.over_y()
    for made in last_loads:
        made.wait()
    for made in back + w_cores:
        made.wait_recv()

    mixed = emb_in[...].reshape(128, 768).astype(F32)
    for h in range(2):
        context_half = crecv[2 * h : 2 * h + 2].reshape(128, 384)
        made = [
            jnp.dot(
                context_half,
                wrbuf[n, 2 * h : 2 * h + 2].reshape(384, 384),
                preferred_element_type=F32,
            )
            for n in range(2)
        ]
        mixed = mixed + jnp.concatenate(made, axis=1)
    resid[...] = mixed
    center = mixed - jnp.mean(mixed, axis=-1, keepdims=True)
    variance = jnp.mean(center * center, axis=-1, keepdims=True)
    normed = (center * lax.rsqrt(variance + 1e-05) * gain_in[...].reshape(1, 768)).astype(BF16)
    above = lax.broadcasted_iota(jnp.int32, (128, 128), 0)
    along = lax.broadcasted_iota(jnp.int32, (128, 128), 1)
    column_at = above // 16 % 4 * 2 + above // 64
    turn = (along == (above % 16) * 8 + column_at).astype(F32).astype(BF16)
    turned = jnp.dot(turn, normed, preferred_element_type=F32).astype(BF16)
    nsend[...] = turned.reshape(2, 4, 16, 768)

    pair = me.x // 2
    x_mate = (me.x // 2) * 2 + 1 - me.x % 2
    x_over = 3 - me.x
    mate, over = me.at(x=x_mate), me.at(x=x_over)
    crossed = links.copy(nsend.at[1 - pair], xr, over)
    order = (2, 1, 3)

    def there(d):
        return (me.zh + d) % 4

    own = [
        links.copy(nsend.at[pair, there(d)], nb.at[me.x, me.co, me.zh], me.at(zh=there(d)))
        for d in order
    ]
    nb[me.x, me.co, me.zh] = nsend[pair, me.zh]
    crossed.wait_recv()
    far = [
        links.copy(xr.at[there(d)], nb.at[x_over, me.co, me.zh], me.at(zh=there(d))) for d in order
    ]
    nb[x_over, me.co, me.zh] = xr[me.zh]
    w_q.far_y()
    w_q_core = w_q.to_core(core, core_half)
    w_c.relay_y()
    for made in own:
        made.wait_recv()
    piece = nb.at[me.x, me.co]
    to_mate = [links.copy(piece, piece, mate)]
    to_core = [links.copy(piece, piece, core)]
    for n, d in ((None, 0), (1, 1), (2, 3), (0, 2)):
        if n is not None:
            far[n].wait_recv()
        piece = nb.at[x_over, me.co, (me.zh + 4 - d) % 4]
        to_mate.append(links.copy(piece, piece, mate))
        to_core.append(links.copy(piece, piece, core))
    to_mate[0].wait_recv()
    piece = nb.at[x_mate, me.co]
    to_core.append(links.copy(piece, piece, core))
    for n, d in enumerate((0, 1, 3, 2)):
        to_mate[n + 1].wait_recv()
        piece = nb.at[3 - x_mate, me.co, (me.zh + 4 - d) % 4]
        to_core.append(links.copy(piece, piece, core))
    w_c.far_y()
    w_c_core = w_c.to_core(core, slice(None))
    w_q_core.wait_recv()
    for made in marks + to_core:
        made.wait_recv()

    tokens = nb[...].reshape(512, 768)
    w_kv = wqbuf[:, :, :, :, 384:1152].reshape(768, 768)
    keys_values = jnp.dot(tokens, w_kv, preferred_element_type=F32).astype(BF16)
    for p in range(3):
        kc[p] = keys_values[:, 128 * p : 128 * p + 128]
        vc[p] = keys_values[:, 384 + 128 * p : 512 + 128 * p]
    asking = nb[:, me.co].reshape(256, 768)
    w_queries = wqbuf[:, :, :, :, 0:384].reshape(768, 384)
    queries = jnp.dot(asking, w_queries, preferred_element_type=F32).astype(BF16)
    for p in range(3):
        qc[p] = queries[:, 128 * p : 128 * p + 128]

    everywhere = jnp.concatenate([mx[x] for x in range(4)], axis=1)
    column = lax.broadcasted_iota(jnp.int32, (8, 512), 0) == 2 * me.zh + pair
    keep = jnp.sum(jnp.where(column, everywhere, 0.0), axis=0, keepdims=True) > 0

    def attend(p, carry):
        k, v = kc[p], vc[p]
        for b in range(4):
            q = qc[p, 64 * b : 64 * b + 64]
            both = jnp.concatenate([q * low_b, q * high_b], axis=0)
            scores = lax.dot_general(
                both, k, (((1,), (1,)), ((), ())), preferred_element_type=F32
            ) * (1.0 / math.sqrt(DH))
            scores = jnp.where(keep, scores, -1000000000.0)
            grown = jnp.exp(scores - jnp.max(scores, axis=1, keepdims=True))
            size = jnp.sum(grown, axis=1, keepdims=True)
            made = jnp.dot(grown.astype(BF16), v, preferred_element_type=F32) / size
            made = jnp.where(low, made[:64], made[64:]).astype(BF16)
            asend[b, p] = made.reshape(4, 16, 128)
        return carry

    lax.fori_loop(0, 3, attend, 0)

    mine = 2 * me.zh + pair
    backs = []
    for d in (2, 1, 3, 0):
        zh = (me.zh + d) % 4
        for e in (2, 1, 3, 0):
            if d == e == 0:
                continue
            x = (me.x + e) % 4
            backs.append(
                links.copy(asend.at[x, :, zh], arecv.at[mine, me.x % 2], me.at(x=x, zh=zh))
            )
    arecv[mine, me.x % 2] = asend[me.x, :, me.zh]
    for made in backs:
        made.wait_recv()
    w_c_core.wait_recv()
    turn_back = (above == (along % 16) * 8 + along // 16).astype(F32).astype(BF16)
    attended = jnp.concatenate(
        [arecv[:, h, p].reshape(128, 128) for h in range(2) for p in range(3)], axis=1
    )
    attended = jnp.dot(turn_back, attended, preferred_element_type=F32).astype(BF16)
    for n in range(2):
        out[:, 384 * n : 384 * n + 384] = resid[:, 384 * n : 384 * n + 384] + jnp.dot(
            attended, wcbuf[n].reshape(768, 384), preferred_element_type=F32
        )
    links.finish()


def per_device(emb, trip, occ, wr, wq, wc, gain):
    vmem = pl.BlockSpec(memory_space=pltpu.VMEM)
    n = 160
    out = pl.pallas_call(
        layer_kernel,
        out_shape=jax.ShapeDtypeStruct((128, 768), F32),
        in_specs=[pl.BlockSpec(memory_space=pl.ANY)] * 7,
        out_specs=vmem,
        scratch_shapes=[
            pltpu.VMEM((16, 8, 768), BF16),
            pltpu.VMEM((16, 8, 768), BF16),
            pltpu.VMEM((4, 4, 8, 8, 384), BF16),
            pltpu.VMEM((4, 4, 8, 8, 384), BF16),
            pltpu.VMEM((4, 8, 8, 384), BF16),
            pltpu.VMEM((16, 12, 128), F32),
            pltpu.VMEM((16, 12, 128), F32),
            pltpu.VMEM((4, 12, 128), F32),
            pltpu.VMEM((16, 12, 128), F32),
            pltpu.VMEM((4, 8, 8, 384), BF16),
            pltpu.VMEM((4, 8, 8, 384), BF16),
            pltpu.VMEM((2, 4, 4, 6, 8, 384), BF16),
            pltpu.VMEM((2, 4, 4, 6, 8, 384), BF16),
            pltpu.VMEM((4, 4, 6, 8, 1152), BF16),
            pltpu.VMEM((8, 8, 128), F32),
            pltpu.VMEM((4, 8, 128), F32),
            pltpu.VMEM((128, 768), F32),
            pltpu.VMEM((2, 4, 16, 768), BF16),
            pltpu.VMEM((4, 16, 768), BF16),
            pltpu.VMEM((4, 2, 4, 16, 768), BF16),
            pltpu.VMEM((3, 512, 128), BF16),
            pltpu.VMEM((3, 512, 128), BF16),
            pltpu.VMEM((3, 256, 128), BF16),
            pltpu.VMEM((4, 3, 4, 16, 128), BF16),
            pltpu.VMEM((8, 2, 3, 16, 128), BF16),
            pltpu.VMEM((8, 16), jnp.int32),
            pltpu.VMEM((16, 8, 768), BF16),
            pltpu.VMEM((768,), F32),
            pltpu.SemaphoreType.DMA((n,)),
            pltpu.SemaphoreType.DMA((n,)),
            pltpu.SemaphoreType.DMA((12,)),
        ],
        compiler_params=pltpu.CompilerParams(
            collective_id=1, has_side_effects=True, vmem_limit_bytes=56 * 1024 * 1024
        ),
        name="msa_layer",
    )(
        emb,
        trip,
        occ.T,
        wr.reshape(6, 8, 768),
        wq.reshape(6, 8, 2304),
        wc.reshape(6, 8, 768),
        gain,
    )
    return out.reshape(16, 8, 768)


def solution(mesh):
    both = P("seq", "col", None)
    return jax.shard_map(
        per_device,
        mesh=mesh,
        in_specs=(both, both, P("seq", "col"), P("col", None), P("col", None), P("col", None), P()),
        out_specs=both,
        check_vma=False,
    )
```

```python
import functools
import math

import jax
import jax.numpy as jnp
from jax import lax
from jax.experimental import pallas as pl
from jax.experimental.pallas import tpu as pltpu
from jax.sharding import Mesh
from jax.sharding import PartitionSpec as P

H = 12
DH = 64
F32 = jnp.float32
BF16 = jnp.bfloat16
MESH = pl.DeviceIdType.MESH


class Group:
    def __init__(self, links, whole):
        self.links, self.whole, self.k = links, whole, links.count
        links.count += 1
        links.started.append(self)

    def add(self, src, dst, device):
        pltpu.make_async_remote_copy(
            src_ref=src,
            dst_ref=dst,
            send_sem=self.links.send_sem.at[self.k],
            recv_sem=self.links.recv_sem.at[self.k],
            device_id=device,
            device_id_type=MESH,
        ).start()

    def wait_recv(self):
        pltpu.make_async_copy(self.whole, self.whole, self.links.recv_sem.at[self.k]).wait()

    def wait_send(self):
        pltpu.make_async_copy(self.whole, self.whole, self.links.send_sem.at[self.k]).wait()


class Links:
    def __init__(self, send_sem, recv_sem):
        self.send_sem, self.recv_sem, self.count, self.started = send_sem, recv_sem, 0, []

    def copy(self, src, dst, device):
        k = self.count
        self.count += 1
        made = pltpu.make_async_remote_copy(
            src_ref=src,
            dst_ref=dst,
            send_sem=self.send_sem.at[k],
            recv_sem=self.recv_sem.at[k],
            device_id=device,
            device_id_type=MESH,
        )
        made.start()
        self.started.append(made)
        return made

    def finish(self):
        for made in self.started:
            made.wait_send()


class Place:
    def __init__(self):
        s, c = lax.axis_index("seq"), lax.axis_index("col")
        self.x, self.zh, self.co = s // 8, (s // 2) % 4, s % 2
        self.y, self.zl = c // 4, c % 4

    def at(self, **moved):
        g = {k: moved.get(k, getattr(self, k)) for k in ("x", "zh", "co", "y", "zl")}
        return (g["x"] * 8 + g["zh"] * 2 + g["co"], g["y"] * 4 + g["zl"])

    def group(self):
        return self.x * 4 + self.co * 2 + self.zl % 2

    def in_group(self, d):
        g = (self.group() + d) % 16
        return g, self.at(x=g // 4, co=(g // 2) % 2, zl=(self.zl // 2) * 2 + g % 2)


def meet(devices):
    barrier = pltpu.get_barrier_semaphore()
    for device in devices:
        pl.semaphore_signal(barrier, inc=1, device_id=device, device_id_type=MESH)
    pl.semaphore_wait(barrier, len(devices))


class Weights:
    def __init__(self, me, links, buf, rows, up, down):
        self.me, self.links, self.buf, self.rows, self.up, self.down = me, links, buf, rows, up, down
        self.y_up, self.y_down, self.y_far = (me.y + 1) % 4, (me.y + 3) % 4, (me.y + 2) % 4
        self.right, self.left = me.at(x=(me.x + 1) % 4), me.at(x=(me.x + 3) % 4)

    def send(self, piece, device):
        return self.links.copy(piece, piece, device)

    def over_z(self):
        piece = self.buf.at[self.me.y, self.me.zl, self.rows]
        self.z = Group(self.links, self.buf.at[0, 0:3, self.rows])
        for d in (1, 3, 2):
            self.z.add(piece, piece, self.me.at(zl=(self.me.zl + d) % 4))

    def over_y(self):
        self.z.wait_recv()
        piece = self.buf.at[self.me.y, :, self.rows]
        self.ups = self.send(piece, self.up)
        self.downs = self.send(piece, self.down)

    def relay_y(self):
        self.far = Group(self.links, self.buf.at[0, :, self.rows])
        self.ups.wait_recv()
        piece = self.buf.at[self.y_down, 0:2, self.rows]
        self.far.add(piece, piece, self.up)
        self.downs.wait_recv()
        piece = self.buf.at[self.y_up, 2:4, self.rows]
        self.far.add(piece, piece, self.down)

    def near_x(self):
        self.xs = Group(self.links, self.buf.at[:, :, self.rows])
        for y, device in ((self.me.y, self.right), (self.y_up, self.right), (self.y_down, self.left)):
            piece = self.buf.at[y, :, self.rows]
            self.xs.add(piece, piece, device)

    def far_y(self):
        self.far.wait_recv()

    def far_x(self):
        piece = self.buf.at[self.y_far, :, self.rows]
        self.xs.add(piece, piece, self.left)

    def arrive(self):
        self.xs.wait_recv()

    def to_core(self, core, rows):
        return self.send(self.buf.at[:, :, rows], core)


class Ring:
    def __init__(self, me, links, buf, up, down):
        self.me, self.links, self.buf, self.up, self.down = me, links, buf, up, down
        self.ups, self.downs = {}, {}
        self.rest = Group(links, buf.at[0:2])

    def send(self, d):
        piece = self.buf.at[self.me.y, (self.me.zl + 4 - d) % 4]
        if d < 2:
            self.ups[d] = self.links.copy(piece, piece, self.up)
            self.rest.add(piece, piece, self.down)
        else:
            self.rest.add(piece, piece, self.up)
            self.downs[d] = self.links.copy(piece, piece, self.down)


def layer_kernel(
    emb, trip, occ, wr, wq, wc, gain, out,
    qraw, qs, kbuf, vbuf, qbuf, lsend, lrecv, erecv, pbuf, csend, crecv,
    wrbuf, wcbuf, wqbuf, mslot, mx, resid, nsend, xr, nb, kc, vc, qc, asend, arecv,
    occ_in, emb_in, gain_in, send_sem, recv_sem, load_sem,
):
    me = Place()
    links = Links(send_sem, recv_sem)
    along_z = [((me.zl + d) % 4, me.at(zl=(me.zl + d) % 4)) for d in range(1, 4)]
    y_up, y_down = (me.y + 1) % 4, (me.y + 3) % 4
    up, down = me.at(y=y_up), me.at(y=y_down)
    everyone = [d for _, d in along_z] + [up, down] + [me.in_group(d)[1] for d in range(1, 16)]
    for d in range(1, 4):
        zh = (me.zh + d) % 4
        for e in range(4):
            everyone.append(me.at(zh=zh, x=(me.x + e) % 4))

    loads = []

    def load(src, dst):
        made = pltpu.make_async_copy(src, dst, load_sem.at[len(loads)])
        made.start()
        loads.append(made)
        return made

    def share(z, first):
        return (
            pl.ds(pl.multiple_of((z % 2) * 8, 8), 8),
            slice(None),
            pl.ds(pl.multiple_of(first + (z // 2) * 384, 128), 384),
        )

    half, other_half = pl.ds(3 * (me.x % 2), 3), pl.ds(3 - 3 * (me.x % 2), 3)
    w_r = Weights(me, links, wrbuf.at[me.co], half, up, down)
    w_c = Weights(me, links, wcbuf.at[me.co], slice(None), up, down)
    core_half = pl.ds(3 * me.co, 3)
    w_q = Weights(me, links, wqbuf, core_half, up, down)
    core = me.at(co=1 - me.co)
    half_lanes = pl.ds(pl.multiple_of(384 * me.co, 128), 384)
    q_loads = [load(trip.at[:, :, 0:768], qraw), load(occ, occ_in)]
    k_load = load(trip.at[share(me.zl, 768)], kbuf.at[me.y, me.zl])
    w_loads = [
        load(wr.at[half, :, half_lanes], wrbuf.at[me.co, me.y, me.zl, half]),
        load(wc.at[:, :, half_lanes], wcbuf.at[me.co, me.y, me.zl]),
    ]
    for t in range(3):
        at = pl.ds(pl.multiple_of(768 * t + 384 * (me.x % 2), 128), 384)
        w_loads.append(
            load(
                wq.at[core_half, :, at],
                wqbuf.at[me.y, me.zl, core_half, :, 384 * t : 384 * t + 384],
            )
        )
    v_load = load(trip.at[share(me.zl, 1536)], vbuf.at[me.y, me.zl])
    last_loads = [load(emb, emb_in), load(gain, gain_in)]

    meet(everyone)

    kz = [links.copy(trip.at[share(z, 768)], kbuf.at[me.y, me.zl], dev) for z, dev in along_z]
    k_load.wait()
    kring = Ring(me, links, kbuf, up, down)
    kring.send(0)

    for made in q_loads:
        made.wait()
    rows = lax.broadcasted_iota(jnp.int32, (128, 16), 0)
    seqs = lax.broadcasted_iota(jnp.int32, (128, 16), 1)
    occupied = occ_in[...].astype(F32).astype(BF16)
    spread = lax.dot_general(
        (rows // 8 == seqs).astype(F32).astype(BF16),
        occupied,
        (((1,), (1,)), ((), ())),
        preferred_element_type=F32,
    )
    picked = lax.broadcasted_iota(jnp.int32, (128, 8), 0) % 8 == lax.broadcasted_iota(
        jnp.int32, (128, 8), 1
    )
    live = jnp.sum(jnp.where(picked, spread, 0.0), axis=1, keepdims=True)
    query = qraw[...].reshape(128, 768).astype(F32) * live
    qs[...] = query.astype(BF16).reshape(16, 8, 768)
    qz = Group(links, qbuf.at[0:3])
    for z, dev in along_z:
        qz.add(qs.at[share(z, 0)], qbuf.at[me.zl], dev)
    for made in w_loads:
        made.wait()
    w_r.over_z()
    qbuf[me.zl] = qs[share(me.zl, 0)]

    lane = lax.broadcasted_iota(jnp.int32, (16, 128), 1)
    mine = (lane % 16 == lax.broadcasted_iota(jnp.int32, (16, 128), 0)) & (
        lane // 16 == me.co * 4 + me.zh
    )
    mslot[me.zh] = jnp.dot(
        occupied, mine.astype(F32).astype(BF16), preferred_element_type=F32
    )
    marks = Group(links, mslot.at[0:3])
    for d in range(1, 4):
        marks.add(mslot.at[me.zh], mslot.at[me.zh], me.at(zh=(me.zh + d) % 4))

    def around_y(buf, arrivals, ring):
        for d in range(1, 4):
            arrivals[d - 1].wait_recv()
            ring.send(d)

    def relay_y(buf, ring):
        for d in range(2):
            ring.ups[d].wait_recv()
            piece = buf.at[y_down, (me.zl + 4 - d) % 4]
            ring.rest.add(piece, piece, up)
            ring.downs[d + 2].wait_recv()
            piece = buf.at[y_up, (me.zl + 4 - d - 2) % 4]
            ring.rest.add(piece, piece, down)
        return [ring.rest]

    around_y(kbuf, kz, kring)
    vz = [links.copy(trip.at[share(z, 1536)], vbuf.at[me.y, me.zl], dev) for z, dev in along_z]
    rest = relay_y(kbuf, kring)
    w_r.over_y()
    qz.wait_recv()
    for k in rest:
        k.wait_recv()

    low = lax.broadcasted_iota(jnp.int32, (1, 128), 1) < 64
    low_b, high_b = low.astype(F32).astype(BF16), 1.0 - low.astype(F32)
    high_b = high_b.astype(BF16)

    def add_logits(r, totals):
        q = qbuf[:, r].reshape(32, 384)
        k = kbuf[:, :, r].reshape(128, 384)
        new = []
        for p in range(3):
            mine = q[:, 128 * p : 128 * p + 128]
            both = jnp.concatenate([mine * low_b, mine * high_b], axis=0)
            new.append(
                totals[p]
                + lax.dot_general(
                    both,
                    k[:, 128 * p : 128 * p + 128],
                    (((1,), (1,)), ((), ())),
                    preferred_element_type=F32,
                )
            )
        return tuple(new)

    totals = lax.fori_loop(0, 8, add_logits, (jnp.zeros((64, 128), F32),) * 3)
    scale = 1.0 / (math.sqrt(DH) * math.sqrt(512))
    logits = jnp.concatenate(totals, axis=0) * scale
    for g in range(16):
        lsend[g] = logits[12 * g : 12 * g + 12]
    parts = Group(links, lrecv.at[0:15])
    for d in range(1, 16):
        g, dev = me.in_group(d)
        parts.add(lsend.at[g], lrecv.at[me.group()], dev)
    lrecv[me.group()] = lsend[me.group()]
    v_load.wait()
    vring = Ring(me, links, vbuf, up, down)
    vring.send(0)
    around_y(vbuf, vz, vring)
    parts.wait_recv()
    total = lrecv[0]
    for g in range(1, 16):
        total = total + lrecv[g]
    erecv[me.zh] = total
    parts = Group(links, erecv.at[0:3])
    for d in (2, 1, 3):
        slot = erecv.at[me.zh]
        parts.add(slot, slot, me.at(zh=(me.zh + d) % 4))
    w_r.relay_y()
    w_r.near_x()
    parts.wait_recv()
    total = erecv[0]
    for e in range(1, 4):
        total = total + erecv[e]
    top = jnp.max(total, axis=1, keepdims=True)
    grown = jnp.exp(total - top)
    pbuf[me.group()] = grown / jnp.sum(grown, axis=1, keepdims=True)
    parts = Group(links, pbuf.at[0:15])
    for d in range(1, 16):
        _, dev = me.in_group(d)
        slot = pbuf.at[me.group()]
        parts.add(slot, slot, dev)
    vrest = relay_y(vbuf, vring)
    w_q.over_z()
    w_c.over_z()
    w_r.far_y()
    w_r.far_x()
    w_cores = [w_r.to_core(core, half)]
    marks.wait_recv()
    mx[me.x * 2 + me.co] = mslot[0] + mslot[1] + mslot[2] + mslot[3]
    marks = Group(links, mx.at[0:7])
    slot = mx.at[me.x * 2 + me.co]
    for d in range(1, 8):
        g = (me.x * 2 + me.co + d) % 8
        marks.add(slot, slot, me.at(x=g // 2, co=g % 2))
    for part in vrest + [parts]:
        part.wait_recv()
    all_probs = jnp.concatenate([pbuf[g] for g in range(16)], axis=0).astype(BF16)

    def context(r, carry):
        v = vbuf[:, :, r].reshape(128, 384)
        made = []
        for p in range(3):
            both = jnp.dot(
                all_probs[64 * p : 64 * p + 64],
                v[:, 128 * p : 128 * p + 128],
                preferred_element_type=F32,
            )
            made.append(jnp.where(low, both[:32], both[32:]))
        csend[:, r] = jnp.concatenate(made, axis=1).astype(BF16).reshape(4, 8, 384)
        return carry

    lax.fori_loop(0, 8, context, 0)
    back = Group(links, crecv.at[0:3])
    for z, dev in along_z:
        back.add(csend.at[z], crecv.at[me.zl], dev)
    crecv[me.zl] = csend[me.zl]
    w_r.arrive()
    w_cores.append(w_r.to_core(core, other_half))
    w_q.over_y()
    for made in last_loads:
        made.wait()
    for made in [back] + w_cores:
        made.wait_recv()

    mixed = emb_in[...].reshape(128, 768).astype(F32)
    for h in range(2):
        context_half = crecv[2 * h : 2 * h + 2].reshape(128, 384)
        made = [
            jnp.dot(
                context_half,
                wrbuf[n, 2 * h : 2 * h + 2].reshape(384, 384),
                preferred_element_type=F32,
            )
            for n in range(2)
        ]
        mixed = mixed + jnp.concatenate(made, axis=1)
    resid[...] = mixed
    center = mixed - jnp.mean(mixed, axis=-1, keepdims=True)
    variance = jnp.mean(center * center, axis=-1, keepdims=True)
    normed = (center * lax.rsqrt(variance + 1e-05) * gain_in[...].reshape(1, 768)).astype(BF16)
    above = lax.broadcasted_iota(jnp.int32, (128, 128), 0)
    along = lax.broadcasted_iota(jnp.int32, (128, 128), 1)
    column_at = above // 16 % 4 * 2 + above // 64
    turn = (along == (above % 16) * 8 + column_at).astype(F32).astype(BF16)
    turned = jnp.dot(turn, normed, preferred_element_type=F32).astype(BF16)
    nsend[...] = turned.reshape(2, 4, 16, 768)

    pair = me.x // 2
    x_mate = (me.x // 2) * 2 + 1 - me.x % 2
    x_over = 3 - me.x
    mate, over = me.at(x=x_mate), me.at(x=x_over)
    crossed = links.copy(nsend.at[1 - pair], xr, over)
    order = (2, 1, 3)

    def there(d):
        return (me.zh + d) % 4

    own = Group(links, nb.at[0, 0, 0:3])
    for d in order:
        own.add(nsend.at[pair, there(d)], nb.at[me.x, me.co, me.zh], me.at(zh=there(d)))
    nb[me.x, me.co, me.zh] = nsend[pair, me.zh]
    crossed.wait_recv()
    far = [
        links.copy(xr.at[there(d)], nb.at[x_over, me.co, me.zh], me.at(zh=there(d))) for d in order
    ]
    nb[x_over, me.co, me.zh] = xr[me.zh]
    w_q.relay_y()
    w_c.over_y()
    own.wait_recv()
    piece = nb.at[me.x, me.co]
    to_mate = [links.copy(piece, piece, mate)]
    to_core = Group(links, nb.at[:, 0])
    to_core.add(piece, piece, core)
    for n, d in ((None, 0), (1, 1), (2, 3), (0, 2)):
        if n is not None:
            far[n].wait_recv()
        piece = nb.at[x_over, me.co, (me.zh + 4 - d) % 4]
        to_mate.append(links.copy(piece, piece, mate))
        to_core.add(piece, piece, core)
    w_q.far_y()
    w_q_core = w_q.to_core(core, core_half)
    w_c.relay_y()
    to_mate[0].wait_recv()
    piece = nb.at[x_mate, me.co]
    to_core.add(piece, piece, core)
    for n, d in enumerate((0, 1, 3, 2)):
        to_mate[n + 1].wait_recv()
        piece = nb.at[3 - x_mate, me.co, (me.zh + 4 - d) % 4]
        to_core.add(piece, piece, core)
    w_q_core.wait_recv()
    marks.wait_recv()
    to_core.wait_recv()

    tokens = nb[...].reshape(512, 768)
    w_kv = wqbuf[:, :, :, :, 384:1152].reshape(768, 768)
    keys_values = jnp.dot(tokens, w_kv, preferred_element_type=F32).astype(BF16)
    for p in range(3):
        kc[p] = keys_values[:, 128 * p : 128 * p + 128]
        vc[p] = keys_values[:, 384 + 128 * p : 512 + 128 * p]
    asking = nb[:, me.co].reshape(256, 768)
    w_queries = wqbuf[:, :, :, :, 0:384].reshape(768, 384)
    queries = jnp.dot(asking, w_queries, preferred_element_type=F32).astype(BF16)
    for p in range(3):
        qc[p] = queries[:, 128 * p : 128 * p + 128]

    everywhere = jnp.concatenate([mx[2 * x] + mx[2 * x + 1] for x in range(4)], axis=1)
    column = lax.broadcasted_iota(jnp.int32, (8, 512), 0) == 2 * me.zh + pair
    keep = jnp.sum(jnp.where(column, everywhere, 0.0), axis=0, keepdims=True) > 0

    mine = 8 * (me.x % 2) + 2 * me.zh + pair
    backs = Group(links, arecv.at[0:15])
    for e in (2, 1, 3, 0):
        x = (me.x + e) % 4
        for p in range(3):
            q = qc[p, pl.ds(pl.multiple_of(64 * x, 64), 64)]
            both = jnp.concatenate([q * low_b, q * high_b], axis=0)
            scores = lax.dot_general(
                both, kc[p], (((1,), (1,)), ((), ())), preferred_element_type=F32
            ) * (1.0 / math.sqrt(DH))
            scores = jnp.where(keep, scores, -1000000000.0)
            grown = jnp.exp(scores - jnp.max(scores, axis=1, keepdims=True))
            size = jnp.sum(grown, axis=1, keepdims=True)
            made = jnp.dot(grown.astype(BF16), vc[p], preferred_element_type=F32) / size
            made = jnp.where(low, made[:64], made[64:]).astype(BF16)
            asend[x, p] = made.reshape(4, 16, 128)
        for d in (2, 1, 3, 0):
            if d == e == 0:
                continue
            zh = (me.zh + d) % 4
            backs.add(asend.at[x, :, zh], arecv.at[mine], me.at(x=x, zh=zh))
    w_c.far_y()
    w_c_core = w_c.to_core(core, slice(None))
    arecv[mine] = asend[me.x, :, me.zh]
    backs.wait_recv()
    w_c_core.wait_recv()
    turn_back = (above == (along % 16) * 8 + along // 16).astype(F32).astype(BF16)
    attended = jnp.concatenate(
        [arecv[8 * h : 8 * h + 8, p].reshape(128, 128) for h in range(2) for p in range(3)], axis=1
    )
    attended = jnp.dot(turn_back, attended, preferred_element_type=F32).astype(BF16)
    for n in range(2):
        out[:, 384 * n : 384 * n + 384] = resid[:, 384 * n : 384 * n + 384] + jnp.dot(
            attended, wcbuf[n].reshape(768, 384), preferred_element_type=F32
        )
    links.finish()


def per_device(emb, trip, occ, wr, wq, wc, gain):
    vmem = pl.BlockSpec(memory_space=pltpu.VMEM)
    n = 52
    out = pl.pallas_call(
        layer_kernel,
        out_shape=jax.ShapeDtypeStruct((128, 768), F32),
        in_specs=[pl.BlockSpec(memory_space=pl.ANY)] * 7,
        out_specs=vmem,
        scratch_shapes=[
            pltpu.VMEM((16, 8, 768), BF16),
            pltpu.VMEM((16, 8, 768), BF16),
            pltpu.VMEM((4, 4, 8, 8, 384), BF16),
            pltpu.VMEM((4, 4, 8, 8, 384), BF16),
            pltpu.VMEM((4, 8, 8, 384), BF16),
            pltpu.VMEM((16, 12, 128), F32),
            pltpu.VMEM((16, 12, 128), F32),
            pltpu.VMEM((4, 12, 128), F32),
            pltpu.VMEM((16, 12, 128), F32),
            pltpu.VMEM((4, 8, 8, 384), BF16),
            pltpu.VMEM((4, 8, 8, 384), BF16),
            pltpu.VMEM((2, 4, 4, 6, 8, 384), BF16),
            pltpu.VMEM((2, 4, 4, 6, 8, 384), BF16),
            pltpu.VMEM((4, 4, 6, 8, 1152), BF16),
            pltpu.VMEM((4, 8, 128), F32),
            pltpu.VMEM((8, 8, 128), F32),
            pltpu.VMEM((128, 768), F32),
            pltpu.VMEM((2, 4, 16, 768), BF16),
            pltpu.VMEM((4, 16, 768), BF16),
            pltpu.VMEM((4, 2, 4, 16, 768), BF16),
            pltpu.VMEM((3, 512, 128), BF16),
            pltpu.VMEM((3, 512, 128), BF16),
            pltpu.VMEM((3, 256, 128), BF16),
            pltpu.VMEM((4, 3, 4, 16, 128), BF16),
            pltpu.VMEM((16, 3, 16, 128), BF16),
            pltpu.VMEM((8, 16), jnp.int32),
            pltpu.VMEM((16, 8, 768), BF16),
            pltpu.VMEM((768,), F32),
            pltpu.SemaphoreType.DMA((n,)),
            pltpu.SemaphoreType.DMA((n,)),
            pltpu.SemaphoreType.DMA((12,)),
        ],
        compiler_params=pltpu.CompilerParams(
            collective_id=1, has_side_effects=True, vmem_limit_bytes=56 * 1024 * 1024
        ),
        name="msa_layer",
    )(
        emb,
        trip,
        occ.T,
        wr.reshape(6, 8, 768),
        wq.reshape(6, 8, 2304),
        wc.reshape(6, 8, 768),
        gain,
    )
    return out.reshape(16, 8, 768)


def solution(mesh):
    both = P("seq", "col", None)
    return jax.shard_map(
        per_device,
        mesh=mesh,
        in_specs=(both, both, P("seq", "col"), P("col", None), P("col", None), P("col", None), P()),
        out_specs=both,
        check_vma=False,
    )
```

```python
import functools
import math

import jax
import jax.numpy as jnp
from jax import lax
from jax.experimental import pallas as pl
from jax.experimental.pallas import tpu as pltpu
from jax.sharding import Mesh
from jax.sharding import PartitionSpec as P

H = 12
DH = 64
F32 = jnp.float32
BF16 = jnp.bfloat16
MESH = pl.DeviceIdType.MESH


class Group:
    def __init__(self, links, whole):
        self.links, self.whole, self.k = links, whole, links.count
        links.count += 1
        links.started.append(self)

    def add(self, src, dst, device):
        pltpu.make_async_remote_copy(
            src_ref=src,
            dst_ref=dst,
            send_sem=self.links.send_sem.at[self.k],
            recv_sem=self.links.recv_sem.at[self.k],
            device_id=device,
            device_id_type=MESH,
        ).start()

    def wait_recv(self):
        pltpu.make_async_copy(self.whole, self.whole, self.links.recv_sem.at[self.k]).wait()

    def wait_send(self):
        pltpu.make_async_copy(self.whole, self.whole, self.links.send_sem.at[self.k]).wait()


class Links:
    def __init__(self, send_sem, recv_sem):
        self.send_sem, self.recv_sem, self.count, self.started = send_sem, recv_sem, 0, []

    def copy(self, src, dst, device):
        k = self.count
        self.count += 1
        made = pltpu.make_async_remote_copy(
            src_ref=src,
            dst_ref=dst,
            send_sem=self.send_sem.at[k],
            recv_sem=self.recv_sem.at[k],
            device_id=device,
            device_id_type=MESH,
        )
        made.start()
        self.started.append(made)
        return made

    def finish(self):
        for made in self.started:
            made.wait_send()


class Place:
    def __init__(self):
        s, c = lax.axis_index("seq"), lax.axis_index("col")
        self.x, self.zh, self.co = s // 8, (s // 2) % 4, s % 2
        self.y, self.zl = c // 4, c % 4

    def at(self, **moved):
        g = {k: moved.get(k, getattr(self, k)) for k in ("x", "zh", "co", "y", "zl")}
        return (g["x"] * 8 + g["zh"] * 2 + g["co"], g["y"] * 4 + g["zl"])

    def group(self):
        return self.x * 4 + self.co * 2 + self.zl % 2

    def on_ring(self, d):
        z = (4 * self.zh + self.zl + d + 16) % 16
        return self.at(zh=z // 4, zl=z % 4)

    def in_group(self, d):
        g = (self.group() + d) % 16
        return g, self.at(x=g // 4, co=(g // 2) % 2, zl=(self.zl // 2) * 2 + g % 2)


def meet(devices):
    barrier = pltpu.get_barrier_semaphore()
    for device in devices:
        pl.semaphore_signal(barrier, inc=1, device_id=device, device_id_type=MESH)
    pl.semaphore_wait(barrier, len(devices))


class Weights:
    def __init__(self, me, links, buf, rows, up, down):
        self.me, self.links, self.buf, self.rows, self.up, self.down = me, links, buf, rows, up, down
        self.y_up, self.y_down, self.y_far = (me.y + 1) % 4, (me.y + 3) % 4, (me.y + 2) % 4
        self.right, self.left = me.at(x=(me.x + 1) % 4), me.at(x=(me.x + 3) % 4)

    def send(self, piece, device):
        return self.links.copy(piece, piece, device)

    def over_z(self):
        piece = self.buf.at[self.me.y, self.me.zl, self.rows]
        self.z = Group(self.links, self.buf.at[0, 0:3, self.rows])
        for d in (1, -1, 2):
            self.z.add(piece, piece, self.me.on_ring(d))

    def over_y(self):
        self.z.wait_recv()
        piece = self.buf.at[self.me.y, :, self.rows]
        self.ups = self.send(piece, self.up)
        self.downs = self.send(piece, self.down)

    def relay_y(self):
        self.far = Group(self.links, self.buf.at[0, :, self.rows])
        self.ups.wait_recv()
        piece = self.buf.at[self.y_down, 0:2, self.rows]
        self.far.add(piece, piece, self.up)
        self.downs.wait_recv()
        piece = self.buf.at[self.y_up, 2:4, self.rows]
        self.far.add(piece, piece, self.down)

    def near_x(self):
        self.xs = Group(self.links, self.buf.at[:, :, self.rows])
        for y, device in ((self.me.y, self.right), (self.y_up, self.right), (self.y_down, self.left)):
            piece = self.buf.at[y, :, self.rows]
            self.xs.add(piece, piece, device)

    def far_y(self):
        self.far.wait_recv()

    def far_x(self):
        piece = self.buf.at[self.y_far, :, self.rows]
        self.xs.add(piece, piece, self.left)

    def arrive(self):
        self.xs.wait_recv()

    def to_core(self, core, rows):
        return self.send(self.buf.at[:, :, rows], core)


class Direct:
    def __init__(self, me, links, buf, others):
        self.me, self.links, self.buf, self.others = me, links, buf, others
        self.rest = Group(links, buf.at[0:3])

    def send(self, d):
        piece = self.buf.at[self.me.y, (self.me.zl + 4 - d) % 4]
        for device in self.others:
            self.rest.add(piece, piece, device)


def layer_kernel(
    emb, trip, occ, wr, wq, wc, gain, out,
    qraw, qs, kbuf, vbuf, qbuf, lsend, lrecv, erecv, pbuf, csend, crecv,
    wrbuf, wcbuf, wqbuf, mslot, mx, resid, nsend, xr, nb, kc, vc, qc, asend, arecv,
    occ_in, emb_in, gain_in, send_sem, recv_sem, load_sem,
):
    me = Place()
    links = Links(send_sem, recv_sem)
    along_z = [((me.zl + d) % 4, me.at(zl=(me.zl + d) % 4)) for d in range(1, 4)]
    y_up, y_down = (me.y + 1) % 4, (me.y + 3) % 4
    up, down = me.at(y=y_up), me.at(y=y_down)
    across = me.at(y=(me.y + 2) % 4)
    everyone = [d for _, d in along_z] + [up, down, across] + [me.in_group(d)[1] for d in range(1, 16)]
    everyone += [me.on_ring(d) for d in (1, -1, 2, -2)]
    for d in range(1, 4):
        zh = (me.zh + d) % 4
        for e in range(4):
            everyone.append(me.at(zh=zh, x=(me.x + e) % 4))

    loads = []

    def load(src, dst):
        made = pltpu.make_async_copy(src, dst, load_sem.at[len(loads)])
        made.start()
        loads.append(made)
        return made

    def share(z, first):
        return (
            pl.ds(pl.multiple_of((z % 2) * 8, 8), 8),
            slice(None),
            pl.ds(pl.multiple_of(first + (z // 2) * 384, 128), 384),
        )

    half, other_half = pl.ds(3 * (me.x % 2), 3), pl.ds(3 - 3 * (me.x % 2), 3)
    w_r = Weights(me, links, wrbuf.at[me.co], half, up, down)
    w_c = Weights(me, links, wcbuf.at[me.co], slice(None), up, down)
    core_half = pl.ds(3 * me.co, 3)
    w_q = Weights(me, links, wqbuf, core_half, up, down)
    core = me.at(co=1 - me.co)
    half_lanes = pl.ds(pl.multiple_of(384 * me.co, 128), 384)
    q_loads = [load(trip.at[:, :, 0:768], qraw), load(occ, occ_in)]
    k_load = load(trip.at[share(me.zl, 768)], kbuf.at[me.y, me.zl])
    w_loads = [
        load(wr.at[half, :, half_lanes], wrbuf.at[me.co, me.y, me.zl, half]),
        load(wc.at[:, :, half_lanes], wcbuf.at[me.co, me.y, me.zl]),
    ]
    for t in range(3):
        at = pl.ds(pl.multiple_of(768 * t + 384 * (me.x % 2), 128), 384)
        w_loads.append(
            load(
                wq.at[core_half, :, at],
                wqbuf.at[me.y, me.zl, core_half, :, 384 * t : 384 * t + 384],
            )
        )
    v_load = load(trip.at[share(me.zl, 1536)], vbuf.at[me.y, me.zl])
    last_loads = [load(emb, emb_in), load(gain, gain_in)]

    meet(everyone)

    kz = [links.copy(trip.at[share(z, 768)], kbuf.at[me.y, me.zl], dev) for z, dev in along_z]
    k_load.wait()
    kring = Direct(me, links, kbuf, (across, up, down))
    kring.send(0)

    for made in q_loads:
        made.wait()
    rows = lax.broadcasted_iota(jnp.int32, (128, 16), 0)
    seqs = lax.broadcasted_iota(jnp.int32, (128, 16), 1)
    occupied = occ_in[...].astype(F32).astype(BF16)
    spread = lax.dot_general(
        (rows // 8 == seqs).astype(F32).astype(BF16),
        occupied,
        (((1,), (1,)), ((), ())),
        preferred_element_type=F32,
    )
    picked = lax.broadcasted_iota(jnp.int32, (128, 8), 0) % 8 == lax.broadcasted_iota(
        jnp.int32, (128, 8), 1
    )
    live = jnp.sum(jnp.where(picked, spread, 0.0), axis=1, keepdims=True)
    query = qraw[...].reshape(128, 768).astype(F32) * live
    qs[...] = query.astype(BF16).reshape(16, 8, 768)
    qz = Group(links, qbuf.at[0:3])
    for z, dev in along_z:
        qz.add(qs.at[share(z, 0)], qbuf.at[me.zl], dev)
    for made in w_loads:
        made.wait()
    w_r.over_z()
    qbuf[me.zl] = qs[share(me.zl, 0)]

    lane = lax.broadcasted_iota(jnp.int32, (16, 128), 1)
    mine = (lane % 16 == lax.broadcasted_iota(jnp.int32, (16, 128), 0)) & (
        lane // 16 == me.co * 4 + me.zh
    )
    mslot[me.zh] = jnp.dot(
        occupied, mine.astype(F32).astype(BF16), preferred_element_type=F32
    )
    marks = Group(links, mslot.at[0:3])
    for d in range(1, 4):
        marks.add(mslot.at[me.zh], mslot.at[me.zh], me.at(zh=(me.zh + d) % 4))

    def around_y(buf, arrivals, ring):
        for d in range(1, 4):
            arrivals[d - 1].wait_recv()
            ring.send(d)

    around_y(kbuf, kz, kring)
    vz = [links.copy(trip.at[share(z, 1536)], vbuf.at[me.y, me.zl], dev) for z, dev in along_z]
    rest = [kring.rest]
    w_r.over_y()
    qz.wait_recv()
    for k in rest:
        k.wait_recv()

    low = lax.broadcasted_iota(jnp.int32, (1, 128), 1) < 64
    low_b, high_b = low.astype(F32).astype(BF16), 1.0 - low.astype(F32)
    high_b = high_b.astype(BF16)

    def add_logits(r, totals):
        q = qbuf[:, r].reshape(32, 384)
        k = kbuf[:, :, r].reshape(128, 384)
        new = []
        for p in range(3):
            mine = q[:, 128 * p : 128 * p + 128]
            both = jnp.concatenate([mine * low_b, mine * high_b], axis=0)
            new.append(
                totals[p]
                + lax.dot_general(
                    both,
                    k[:, 128 * p : 128 * p + 128],
                    (((1,), (1,)), ((), ())),
                    preferred_element_type=F32,
                )
            )
        return tuple(new)

    totals = lax.fori_loop(0, 8, add_logits, (jnp.zeros((64, 128), F32),) * 3)
    scale = 1.0 / (math.sqrt(DH) * math.sqrt(512))
    logits = jnp.concatenate(totals, axis=0) * scale
    for g in range(16):
        lsend[g] = logits[12 * g : 12 * g + 12]
    parts = Group(links, lrecv.at[0:15])
    for d in range(1, 16):
        g, dev = me.in_group(d)
        parts.add(lsend.at[g], lrecv.at[me.group()], dev)
    lrecv[me.group()] = lsend[me.group()]
    v_load.wait()
    vring = Direct(me, links, vbuf, (across, up, down))
    vring.send(0)
    around_y(vbuf, vz, vring)
    w_q.over_z()
    w_c.over_z()
    parts.wait_recv()
    total = lrecv[0]
    for g in range(1, 16):
        total = total + lrecv[g]
    erecv[me.zh] = total
    parts = Group(links, erecv.at[0:3])
    for d in (2, 1, 3):
        slot = erecv.at[me.zh]
        parts.add(slot, slot, me.at(zh=(me.zh + d) % 4))
    w_r.relay_y()
    w_r.near_x()
    parts.wait_recv()
    total = erecv[0]
    for e in range(1, 4):
        total = total + erecv[e]
    top = jnp.max(total, axis=1, keepdims=True)
    grown = jnp.exp(total - top)
    pbuf[me.group()] = grown / jnp.sum(grown, axis=1, keepdims=True)
    parts = Group(links, pbuf.at[0:15])
    for d in range(1, 16):
        _, dev = me.in_group(d)
        slot = pbuf.at[me.group()]
        parts.add(slot, slot, dev)
    vrest = [vring.rest]
    w_r.far_y()
    w_r.far_x()
    w_cores = [w_r.to_core(core, half)]
    marks.wait_recv()
    mx[me.x * 2 + me.co] = mslot[0] + mslot[1] + mslot[2] + mslot[3]
    marks = Group(links, mx.at[0:7])
    slot = mx.at[me.x * 2 + me.co]
    for d in range(1, 8):
        g = (me.x * 2 + me.co + d) % 8
        marks.add(slot, slot, me.at(x=g // 2, co=g % 2))
    for part in vrest + [parts]:
        part.wait_recv()
    all_probs = jnp.concatenate([pbuf[g] for g in range(16)], axis=0).astype(BF16)

    def context(r, carry):
        v = vbuf[:, :, r].reshape(128, 384)
        made = []
        for p in range(3):
            both = jnp.dot(
                all_probs[64 * p : 64 * p + 64],
                v[:, 128 * p : 128 * p + 128],
                preferred_element_type=F32,
            )
            made.append(jnp.where(low, both[:32], both[32:]))
        csend[:, r] = jnp.concatenate(made, axis=1).astype(BF16).reshape(4, 8, 384)
        return carry

    lax.fori_loop(0, 8, context, 0)
    back = Group(links, crecv.at[0:3])
    for z, dev in along_z:
        back.add(csend.at[z], crecv.at[me.zl], dev)
    crecv[me.zl] = csend[me.zl]
    w_r.arrive()
    w_cores.append(w_r.to_core(core, other_half))
    w_q.over_y()
    for made in last_loads:
        made.wait()
    for made in [back] + w_cores:
        made.wait_recv()

    mixed = emb_in[...].reshape(128, 768).astype(F32)
    for h in range(2):
        context_half = crecv[2 * h : 2 * h + 2].reshape(128, 384)
        made = [
            jnp.dot(
                context_half,
                wrbuf[n, 2 * h : 2 * h + 2].reshape(384, 384),
                preferred_element_type=F32,
            )
            for n in range(2)
        ]
        mixed = mixed + jnp.concatenate(made, axis=1)
    resid[...] = mixed
    center = mixed - jnp.mean(mixed, axis=-1, keepdims=True)
    variance = jnp.mean(center * center, axis=-1, keepdims=True)
    normed = (center * lax.rsqrt(variance + 1e-05) * gain_in[...].reshape(1, 768)).astype(BF16)
    above = lax.broadcasted_iota(jnp.int32, (128, 128), 0)
    along = lax.broadcasted_iota(jnp.int32, (128, 128), 1)
    column_at = above // 16 % 4 * 2 + above // 64
    turn = (along == (above % 16) * 8 + column_at).astype(F32).astype(BF16)
    turned = jnp.dot(turn, normed, preferred_element_type=F32).astype(BF16)
    nsend[...] = turned.reshape(2, 4, 16, 768)

    pair = me.x // 2
    x_mate = (me.x // 2) * 2 + 1 - me.x % 2
    x_over = 3 - me.x
    mate, over = me.at(x=x_mate), me.at(x=x_over)
    crossed = links.copy(nsend.at[1 - pair], xr, over)
    order = (2, 1, 3)

    def there(d):
        return (me.zh + d) % 4

    own = Group(links, nb.at[0, 0, 0:3])
    for d in order:
        own.add(nsend.at[pair, there(d)], nb.at[me.x, me.co, me.zh], me.at(zh=there(d)))
    nb[me.x, me.co, me.zh] = nsend[pair, me.zh]
    crossed.wait_recv()
    far = [
        links.copy(xr.at[there(d)], nb.at[x_over, me.co, me.zh], me.at(zh=there(d))) for d in order
    ]
    nb[x_over, me.co, me.zh] = xr[me.zh]
    w_q.relay_y()
    w_c.over_y()
    own.wait_recv()
    piece = nb.at[me.x, me.co]
    to_mate = [links.copy(piece, piece, mate)]
    to_core = Group(links, nb.at[:, 0])
    to_core.add(piece, piece, core)
    for n, d in ((None, 0), (1, 1), (2, 3), (0, 2)):
        if n is not None:
            far[n].wait_recv()
        piece = nb.at[x_over, me.co, (me.zh + 4 - d) % 4]
        to_mate.append(links.copy(piece, piece, mate))
        to_core.add(piece, piece, core)
    w_q.far_y()
    w_q_core = w_q.to_core(core, core_half)
    w_c.relay_y()
    to_mate[0].wait_recv()
    piece = nb.at[x_mate, me.co]
    to_core.add(piece, piece, core)
    for n, d in enumerate((0, 1, 3, 2)):
        to_mate[n + 1].wait_recv()
        piece = nb.at[3 - x_mate, me.co, (me.zh + 4 - d) % 4]
        to_core.add(piece, piece, core)
    w_q_core.wait_recv()
    marks.wait_recv()
    to_core.wait_recv()

    tokens = nb[...].reshape(512, 768)
    w_kv = wqbuf[:, :, :, :, 384:1152].reshape(768, 768)
    keys_values = jnp.dot(tokens, w_kv, preferred_element_type=F32).astype(BF16)
    for p in range(3):
        kc[p] = keys_values[:, 128 * p : 128 * p + 128]
        vc[p] = keys_values[:, 384 + 128 * p : 512 + 128 * p]
    asking = nb[:, me.co].reshape(256, 768)
    w_queries = wqbuf[:, :, :, :, 0:384].reshape(768, 384)
    queries = jnp.dot(asking, w_queries, preferred_element_type=F32).astype(BF16)
    for p in range(3):
        qc[p] = queries[:, 128 * p : 128 * p + 128]

    everywhere = jnp.concatenate([mx[2 * x] + mx[2 * x + 1] for x in range(4)], axis=1)
    column = lax.broadcasted_iota(jnp.int32, (8, 512), 0) == 2 * me.zh + pair
    keep = jnp.sum(jnp.where(column, everywhere, 0.0), axis=0, keepdims=True) > 0

    mine = 8 * (me.x % 2) + 2 * me.zh + pair
    backs = Group(links, arecv.at[0:15])
    for e in (2, 1, 3, 0):
        x = (me.x + e) % 4
        for p in range(3):
            q = qc[p, pl.ds(pl.multiple_of(64 * x, 64), 64)]
            both = jnp.concatenate([q * low_b, q * high_b], axis=0)
            scores = lax.dot_general(
                both, kc[p], (((1,), (1,)), ((), ())), preferred_element_type=F32
            ) * (1.0 / math.sqrt(DH))
            scores = jnp.where(keep, scores, -1000000000.0)
            grown = jnp.exp(scores - jnp.max(scores, axis=1, keepdims=True))
            size = jnp.sum(grown, axis=1, keepdims=True)
            made = jnp.dot(grown.astype(BF16), vc[p], preferred_element_type=F32) / size
            made = jnp.where(low, made[:64], made[64:]).astype(BF16)
            asend[x, p] = made.reshape(4, 16, 128)
        for d in (2, 1, 3, 0):
            if d == e == 0:
                continue
            zh = (me.zh + d) % 4
            backs.add(asend.at[x, :, zh], arecv.at[mine], me.at(x=x, zh=zh))
    w_c.far_y()
    w_c_core = w_c.to_core(core, slice(None))
    arecv[mine] = asend[me.x, :, me.zh]
    backs.wait_recv()
    w_c_core.wait_recv()
    turn_back = (above == (along % 16) * 8 + along // 16).astype(F32).astype(BF16)
    attended = jnp.concatenate(
        [arecv[8 * h : 8 * h + 8, p].reshape(128, 128) for h in range(2) for p in range(3)], axis=1
    )
    attended = jnp.dot(turn_back, attended, preferred_element_type=F32).astype(BF16)
    for n in range(2):
        out[:, 384 * n : 384 * n + 384] = resid[:, 384 * n : 384 * n + 384] + jnp.dot(
            attended, wcbuf[n].reshape(768, 384), preferred_element_type=F32
        )
    links.finish()


def per_device(emb, trip, occ, wr, wq, wc, gain):
    vmem = pl.BlockSpec(memory_space=pltpu.VMEM)
    n = 52
    out = pl.pallas_call(
        layer_kernel,
        out_shape=jax.ShapeDtypeStruct((128, 768), F32),
        in_specs=[pl.BlockSpec(memory_space=pl.ANY)] * 7,
        out_specs=vmem,
        scratch_shapes=[
            pltpu.VMEM((16, 8, 768), BF16),
            pltpu.VMEM((16, 8, 768), BF16),
            pltpu.VMEM((4, 4, 8, 8, 384), BF16),
            pltpu.VMEM((4, 4, 8, 8, 384), BF16),
            pltpu.VMEM((4, 8, 8, 384), BF16),
            pltpu.VMEM((16, 12, 128), F32),
            pltpu.VMEM((16, 12, 128), F32),
            pltpu.VMEM((4, 12, 128), F32),
            pltpu.VMEM((16, 12, 128), F32),
            pltpu.VMEM((4, 8, 8, 384), BF16),
            pltpu.VMEM((4, 8, 8, 384), BF16),
            pltpu.VMEM((2, 4, 4, 6, 8, 384), BF16),
            pltpu.VMEM((2, 4, 4, 6, 8, 384), BF16),
            pltpu.VMEM((4, 4, 6, 8, 1152), BF16),
            pltpu.VMEM((4, 8, 128), F32),
            pltpu.VMEM((8, 8, 128), F32),
            pltpu.VMEM((128, 768), F32),
            pltpu.VMEM((2, 4, 16, 768), BF16),
            pltpu.VMEM((4, 16, 768), BF16),
            pltpu.VMEM((4, 2, 4, 16, 768), BF16),
            pltpu.VMEM((3, 512, 128), BF16),
            pltpu.VMEM((3, 512, 128), BF16),
            pltpu.VMEM((3, 256, 128), BF16),
            pltpu.VMEM((4, 3, 4, 16, 128), BF16),
            pltpu.VMEM((16, 3, 16, 128), BF16),
            pltpu.VMEM((8, 16), jnp.int32),
            pltpu.VMEM((16, 8, 768), BF16),
            pltpu.VMEM((768,), F32),
            pltpu.SemaphoreType.DMA((n,)),
            pltpu.SemaphoreType.DMA((n,)),
            pltpu.SemaphoreType.DMA((12,)),
        ],
        compiler_params=pltpu.CompilerParams(
            collective_id=1, has_side_effects=True, vmem_limit_bytes=56 * 1024 * 1024
        ),
        name="msa_layer",
    )(
        emb,
        trip,
        occ.T,
        wr.reshape(6, 8, 768),
        wq.reshape(6, 8, 2304),
        wc.reshape(6, 8, 768),
        gain,
    )
    return out.reshape(16, 8, 768)


def solution(mesh):
    both = P("seq", "col", None)
    return jax.shard_map(
        per_device,
        mesh=mesh,
        in_specs=(both, both, P("seq", "col"), P("col", None), P("col", None), P("col", None), P()),
        out_specs=both,
        check_vma=False,
    )
```

```python
import functools
import math

import jax
import jax.numpy as jnp
from jax import lax
from jax.experimental import pallas as pl
from jax.experimental.pallas import tpu as pltpu
from jax.sharding import Mesh
from jax.sharding import PartitionSpec as P

H = 12
DH = 64
F32 = jnp.float32
BF16 = jnp.bfloat16
MESH = pl.DeviceIdType.MESH


class Group:
    def __init__(self, links, whole):
        self.links, self.whole, self.k = links, whole, links.count
        links.count += 1
        links.started.append(self)

    def add(self, src, dst, device):
        pltpu.make_async_remote_copy(
            src_ref=src,
            dst_ref=dst,
            send_sem=self.links.send_sem.at[self.k],
            recv_sem=self.links.recv_sem.at[self.k],
            device_id=device,
            device_id_type=MESH,
        ).start()

    def wait_recv(self):
        pltpu.make_async_copy(self.whole, self.whole, self.links.recv_sem.at[self.k]).wait()

    def wait_send(self):
        pltpu.make_async_copy(self.whole, self.whole, self.links.send_sem.at[self.k]).wait()


class Links:
    def __init__(self, send_sem, recv_sem):
        self.send_sem, self.recv_sem, self.count, self.started = send_sem, recv_sem, 0, []

    def copy(self, src, dst, device):
        k = self.count
        self.count += 1
        made = pltpu.make_async_remote_copy(
            src_ref=src,
            dst_ref=dst,
            send_sem=self.send_sem.at[k],
            recv_sem=self.recv_sem.at[k],
            device_id=device,
            device_id_type=MESH,
        )
        made.start()
        self.started.append(made)
        return made

    def finish(self):
        for made in self.started:
            made.wait_send()


class Place:
    def __init__(self):
        s, c = lax.axis_index("seq"), lax.axis_index("col")
        self.x, self.zh, self.co = s // 8, (s // 2) % 4, s % 2
        self.y, self.zl = c // 4, c % 4

    def at(self, **moved):
        g = {k: moved.get(k, getattr(self, k)) for k in ("x", "zh", "co", "y", "zl")}
        return (g["x"] * 8 + g["zh"] * 2 + g["co"], g["y"] * 4 + g["zl"])

    def group(self):
        return self.x * 4 + self.co * 2 + self.zl % 2

    def on_ring(self, d):
        z = (4 * self.zh + self.zl + d + 16) % 16
        return self.at(zh=z // 4, zl=z % 4)

    def in_group(self, d):
        g = (self.group() + d) % 16
        return g, self.at(x=g // 4, co=(g // 2) % 2, zl=(self.zl // 2) * 2 + g % 2)


def meet(devices):
    barrier = pltpu.get_barrier_semaphore()
    for device in devices:
        pl.semaphore_signal(barrier, inc=1, device_id=device, device_id_type=MESH)
    pl.semaphore_wait(barrier, len(devices))


class Weights:
    def __init__(self, me, links, buf, rows, up, down):
        self.me, self.links, self.buf, self.rows, self.up, self.down = me, links, buf, rows, up, down
        self.y_up, self.y_down, self.y_far = (me.y + 1) % 4, (me.y + 3) % 4, (me.y + 2) % 4
        self.right, self.left = me.at(x=(me.x + 1) % 4), me.at(x=(me.x + 3) % 4)

    def send(self, piece, device):
        return self.links.copy(piece, piece, device)

    def over_z(self):
        piece = self.buf.at[self.me.y, self.me.zl, self.rows]
        self.z = Group(self.links, self.buf.at[0, 0:3, self.rows])
        for d in (1, -1, 2):
            self.z.add(piece, piece, self.me.on_ring(d))

    def over_y(self):
        self.z.wait_recv()
        piece = self.buf.at[self.me.y, :, self.rows]
        self.ups = self.send(piece, self.up)
        self.downs = self.send(piece, self.down)

    def relay_y(self):
        self.far = Group(self.links, self.buf.at[0, :, self.rows])
        self.ups.wait_recv()
        piece = self.buf.at[self.y_down, 0:2, self.rows]
        self.far.add(piece, piece, self.up)
        self.downs.wait_recv()
        piece = self.buf.at[self.y_up, 2:4, self.rows]
        self.far.add(piece, piece, self.down)

    def near_x(self):
        self.xs = Group(self.links, self.buf.at[:, :, self.rows])
        for y, device in ((self.me.y, self.right), (self.y_up, self.right), (self.y_down, self.left)):
            piece = self.buf.at[y, :, self.rows]
            self.xs.add(piece, piece, device)

    def far_y(self):
        self.far.wait_recv()

    def far_x(self):
        piece = self.buf.at[self.y_far, :, self.rows]
        self.xs.add(piece, piece, self.left)

    def arrive(self):
        self.xs.wait_recv()

    def to_core(self, core, rows):
        return self.send(self.buf.at[:, :, rows], core)


class Direct:
    def __init__(self, me, links, buf, others):
        self.me, self.links, self.buf, self.others = me, links, buf, others
        self.rest = Group(links, buf.at[0:3])

    def send(self, d):
        piece = self.buf.at[self.me.y, (self.me.zl + 4 - d) % 4]
        for device in self.others:
            self.rest.add(piece, piece, device)


def layer_kernel(
    emb, trip, occ, wr, wq, wc, gain, out,
    qraw, qs, kbuf, vbuf, qbuf, lsend, lrecv, erecv, pbuf, csend, crecv,
    wrbuf, wcbuf, wqbuf, mslot, mx, resid, nsend, xr, nb, kc, vc, qc, asend, arecv,
    occ_in, emb_in, gain_in, send_sem, recv_sem, load_sem,
):
    me = Place()
    links = Links(send_sem, recv_sem)
    along_z = [((me.zl + d) % 4, me.at(zl=(me.zl + d) % 4)) for d in range(1, 4)]
    y_up, y_down = (me.y + 1) % 4, (me.y + 3) % 4
    up, down = me.at(y=y_up), me.at(y=y_down)
    across = me.at(y=(me.y + 2) % 4)
    everyone = [d for _, d in along_z] + [up, down, across] + [me.in_group(d)[1] for d in range(1, 16)]
    everyone += [me.on_ring(d) for d in (1, -1, 2, -2)]
    for d in range(1, 4):
        zh = (me.zh + d) % 4
        for e in range(4):
            everyone.append(me.at(zh=zh, x=(me.x + e) % 4))

    loads = []

    def load(src, dst):
        made = pltpu.make_async_copy(src, dst, load_sem.at[len(loads)])
        made.start()
        loads.append(made)
        return made

    def share(z, first):
        return (
            pl.ds(pl.multiple_of((z % 2) * 8, 8), 8),
            slice(None),
            pl.ds(pl.multiple_of(first + (z // 2) * 384, 128), 384),
        )

    half, other_half = pl.ds(3 * (me.x % 2), 3), pl.ds(3 - 3 * (me.x % 2), 3)
    w_r = Weights(me, links, wrbuf.at[me.co], half, up, down)
    w_c = Weights(me, links, wcbuf.at[me.co], slice(None), up, down)
    core_half = pl.ds(3 * me.co, 3)
    w_q = Weights(me, links, wqbuf, core_half, up, down)
    core = me.at(co=1 - me.co)
    half_lanes = pl.ds(pl.multiple_of(384 * me.co, 128), 384)
    q_loads = [load(trip.at[:, :, 0:768], qraw), load(occ, occ_in)]
    k_load = load(trip.at[share(me.zl, 768)], kbuf.at[me.y, me.zl])
    w_loads = [
        load(wr.at[half, :, half_lanes], wrbuf.at[me.co, me.y, me.zl, half]),
        load(wc.at[:, :, half_lanes], wcbuf.at[me.co, me.y, me.zl]),
    ]
    for t in range(3):
        at = pl.ds(pl.multiple_of(768 * t + 384 * (me.x % 2), 128), 384)
        w_loads.append(
            load(
                wq.at[core_half, :, at],
                wqbuf.at[me.y, me.zl, core_half, :, 384 * t : 384 * t + 384],
            )
        )
    v_load = load(trip.at[share(me.zl, 1536)], vbuf.at[me.y, me.zl])
    last_loads = [load(emb, emb_in), load(gain, gain_in)]

    meet(everyone)

    kz = [links.copy(trip.at[share(z, 768)], kbuf.at[me.y, me.zl], dev) for z, dev in along_z]
    k_load.wait()
    kring = Direct(me, links, kbuf, (across, up, down))
    kring.send(0)

    for made in q_loads:
        made.wait()
    rows = lax.broadcasted_iota(jnp.int32, (128, 16), 0)
    seqs = lax.broadcasted_iota(jnp.int32, (128, 16), 1)
    occupied = occ_in[...].astype(F32).astype(BF16)
    spread = lax.dot_general(
        (rows // 8 == seqs).astype(F32).astype(BF16),
        occupied,
        (((1,), (1,)), ((), ())),
        preferred_element_type=F32,
    )
    picked = lax.broadcasted_iota(jnp.int32, (128, 8), 0) % 8 == lax.broadcasted_iota(
        jnp.int32, (128, 8), 1
    )
    live = jnp.sum(jnp.where(picked, spread, 0.0), axis=1, keepdims=True)
    query = qraw[...].reshape(128, 768).astype(F32) * live
    qs[...] = query.astype(BF16).reshape(16, 8, 768)
    qz = Group(links, qbuf.at[0:3])
    for z, dev in along_z:
        qz.add(qs.at[share(z, 0)], qbuf.at[me.zl], dev)
    for made in w_loads:
        made.wait()
    w_r.over_z()
    qbuf[me.zl] = qs[share(me.zl, 0)]

    lane = lax.broadcasted_iota(jnp.int32, (16, 128), 1)
    mine = (lane % 16 == lax.broadcasted_iota(jnp.int32, (16, 128), 0)) & (
        lane // 16 == me.co * 4 + me.zh
    )
    mslot[me.zh] = jnp.dot(
        occupied, mine.astype(F32).astype(BF16), preferred_element_type=F32
    )
    marks = Group(links, mslot.at[0:3])
    for d in range(1, 4):
        marks.add(mslot.at[me.zh], mslot.at[me.zh], me.at(zh=(me.zh + d) % 4))

    def around_y(buf, arrivals, ring):
        for d in range(1, 4):
            arrivals[d - 1].wait_recv()
            ring.send(d)

    around_y(kbuf, kz, kring)
    vz = [links.copy(trip.at[share(z, 1536)], vbuf.at[me.y, me.zl], dev) for z, dev in along_z]
    rest = [kring.rest]
    w_r.over_y()
    qz.wait_recv()
    for k in rest:
        k.wait_recv()

    low = lax.broadcasted_iota(jnp.int32, (1, 128), 1) < 64
    low_b, high_b = low.astype(F32).astype(BF16), 1.0 - low.astype(F32)
    high_b = high_b.astype(BF16)

    def add_logits(r, totals):
        q = qbuf[:, r].reshape(32, 384)
        k = kbuf[:, :, r].reshape(128, 384)
        new = []
        for p in range(3):
            mine = q[:, 128 * p : 128 * p + 128]
            both = jnp.concatenate([mine * low_b, mine * high_b], axis=0)
            new.append(
                totals[p]
                + lax.dot_general(
                    both,
                    k[:, 128 * p : 128 * p + 128],
                    (((1,), (1,)), ((), ())),
                    preferred_element_type=F32,
                )
            )
        return tuple(new)

    totals = lax.fori_loop(0, 8, add_logits, (jnp.zeros((64, 128), F32),) * 3)
    scale = 1.0 / (math.sqrt(DH) * math.sqrt(512))
    logits = jnp.concatenate(totals, axis=0) * scale
    for g in range(16):
        lsend[g] = logits[12 * g : 12 * g + 12]
    parts = Group(links, lrecv.at[0:15])
    for d in range(1, 16):
        g, dev = me.in_group(d)
        parts.add(lsend.at[g], lrecv.at[me.group()], dev)
    lrecv[me.group()] = lsend[me.group()]
    v_load.wait()
    vring = Direct(me, links, vbuf, (across, up, down))
    vring.send(0)
    around_y(vbuf, vz, vring)
    w_q.over_z()
    w_c.over_z()
    parts.wait_recv()
    total = lrecv[0]
    for g in range(1, 16):
        total = total + lrecv[g]
    erecv[me.zh] = total
    parts = Group(links, erecv.at[0:3])
    for d in (2, 1, 3):
        slot = erecv.at[me.zh]
        parts.add(slot, slot, me.at(zh=(me.zh + d) % 4))
    w_r.relay_y()
    w_r.near_x()
    parts.wait_recv()
    total = erecv[0]
    for e in range(1, 4):
        total = total + erecv[e]
    top = jnp.max(total, axis=1, keepdims=True)
    grown = jnp.exp(total - top)
    pbuf[me.group()] = grown / jnp.sum(grown, axis=1, keepdims=True)
    parts = Group(links, pbuf.at[0:15])
    for d in range(1, 16):
        _, dev = me.in_group(d)
        slot = pbuf.at[me.group()]
        parts.add(slot, slot, dev)
    vrest = [vring.rest]
    w_r.far_y()
    w_r.far_x()
    w_cores = [w_r.to_core(core, half)]
    marks.wait_recv()
    mx[me.x * 2 + me.co] = mslot[0] + mslot[1] + mslot[2] + mslot[3]
    marks = Group(links, mx.at[0:7])
    slot = mx.at[me.x * 2 + me.co]
    for d in range(1, 8):
        g = (me.x * 2 + me.co + d) % 8
        marks.add(slot, slot, me.at(x=g // 2, co=g % 2))
    for part in vrest + [parts]:
        part.wait_recv()
    all_probs = jnp.concatenate([pbuf[g] for g in range(16)], axis=0).astype(BF16)

    def context(r, carry):
        v = vbuf[:, :, r].reshape(128, 384)
        made = []
        for p in range(3):
            both = jnp.dot(
                all_probs[64 * p : 64 * p + 64],
                v[:, 128 * p : 128 * p + 128],
                preferred_element_type=F32,
            )
            made.append(jnp.where(low, both[:32], both[32:]))
        csend[:, r] = jnp.concatenate(made, axis=1).astype(BF16).reshape(4, 8, 384)
        return carry

    lax.fori_loop(0, 8, context, 0)
    back = Group(links, crecv.at[0:3])
    for z, dev in along_z:
        back.add(csend.at[z], crecv.at[me.zl], dev)
    crecv[me.zl] = csend[me.zl]
    w_r.arrive()
    w_cores.append(w_r.to_core(core, other_half))
    w_q.over_y()
    for made in last_loads:
        made.wait()
    for made in [back] + w_cores:
        made.wait_recv()

    mixed = emb_in[...].reshape(128, 768).astype(F32)
    for h in range(2):
        context_half = crecv[2 * h : 2 * h + 2].reshape(128, 384)
        made = [
            jnp.dot(
                context_half,
                wrbuf[n, 2 * h : 2 * h + 2].reshape(384, 384),
                preferred_element_type=F32,
            )
            for n in range(2)
        ]
        mixed = mixed + jnp.concatenate(made, axis=1)
    resid[...] = mixed
    center = mixed - jnp.mean(mixed, axis=-1, keepdims=True)
    variance = jnp.mean(center * center, axis=-1, keepdims=True)
    normed = (center * lax.rsqrt(variance + 1e-05) * gain_in[...].reshape(1, 768)).astype(BF16)
    above = lax.broadcasted_iota(jnp.int32, (128, 128), 0)
    along = lax.broadcasted_iota(jnp.int32, (128, 128), 1)
    column_at = above // 16 % 4 * 2 + above // 64
    turn = (along == (above % 16) * 8 + column_at).astype(F32).astype(BF16)
    turned = jnp.dot(turn, normed, preferred_element_type=F32).astype(BF16)
    nsend[...] = turned.reshape(2, 4, 16, 768)

    pair = me.x // 2
    x_mate = (me.x // 2) * 2 + 1 - me.x % 2
    x_over = 3 - me.x
    mate, over = me.at(x=x_mate), me.at(x=x_over)
    mate_core = me.at(x=x_mate, co=1 - me.co)
    crossed = links.copy(nsend.at[1 - pair], xr, over)
    order = (2, 1, 3)

    def there(d):
        return (me.zh + d) % 4

    own = Group(links, nb.at[0, 0, 0:3])
    for d in order:
        own.add(nsend.at[pair, there(d)], nb.at[me.x, me.co, me.zh], me.at(zh=there(d)))
    nb[me.x, me.co, me.zh] = nsend[pair, me.zh]
    crossed.wait_recv()
    far = [
        links.copy(xr.at[there(d)], nb.at[x_over, me.co, me.zh], me.at(zh=there(d))) for d in order
    ]
    nb[x_over, me.co, me.zh] = xr[me.zh]
    w_q.relay_y()
    w_c.over_y()
    own.wait_recv()
    piece = nb.at[me.x, me.co]
    to_mate = [links.copy(piece, piece, mate)]
    to_core = Group(links, nb.at[:, 0])
    to_core.add(piece, piece, core)
    for n, d in ((None, 0), (1, 1), (2, 3), (0, 2)):
        if n is not None:
            far[n].wait_recv()
        piece = nb.at[x_over, me.co, (me.zh + 4 - d) % 4]
        to_mate.append(links.copy(piece, piece, mate))
        to_core.add(piece, piece, mate_core)
        to_core.add(piece, piece, core)
    w_q.far_y()
    w_q_core = w_q.to_core(core, core_half)
    w_c.relay_y()
    to_mate[0].wait_recv()
    piece = nb.at[x_mate, me.co]
    to_core.add(piece, piece, core)
    for made in to_mate[1:]:
        made.wait_recv()
    w_q_core.wait_recv()
    marks.wait_recv()
    to_core.wait_recv()

    tokens = nb[...].reshape(512, 768)
    w_kv = wqbuf[:, :, :, :, 384:1152].reshape(768, 768)
    keys_values = jnp.dot(tokens, w_kv, preferred_element_type=F32).astype(BF16)
    for p in range(3):
        kc[p] = keys_values[:, 128 * p : 128 * p + 128]
        vc[p] = keys_values[:, 384 + 128 * p : 512 + 128 * p]
    asking = nb[:, me.co].reshape(256, 768)
    w_queries = wqbuf[:, :, :, :, 0:384].reshape(768, 384)
    queries = jnp.dot(asking, w_queries, preferred_element_type=F32).astype(BF16)
    for p in range(3):
        qc[p] = queries[:, 128 * p : 128 * p + 128]

    everywhere = jnp.concatenate([mx[2 * x] + mx[2 * x + 1] for x in range(4)], axis=1)
    column = lax.broadcasted_iota(jnp.int32, (8, 512), 0) == 2 * me.zh + pair
    keep = jnp.sum(jnp.where(column, everywhere, 0.0), axis=0, keepdims=True) > 0

    mine = 8 * (me.x % 2) + 2 * me.zh + pair
    backs = Group(links, arecv.at[0:15])
    for e in (2, 1, 3, 0):
        x = (me.x + e) % 4
        for p in range(3):
            q = qc[p, pl.ds(pl.multiple_of(64 * x, 64), 64)]
            both = jnp.concatenate([q * low_b, q * high_b], axis=0)
            scores = lax.dot_general(
                both, kc[p], (((1,), (1,)), ((), ())), preferred_element_type=F32
            ) * (1.0 / math.sqrt(DH))
            scores = jnp.where(keep, scores, -1000000000.0)
            grown = jnp.exp(scores - jnp.max(scores, axis=1, keepdims=True))
            size = jnp.sum(grown, axis=1, keepdims=True)
            made = jnp.dot(grown.astype(BF16), vc[p], preferred_element_type=F32) / size
            made = jnp.where(low, made[:64], made[64:]).astype(BF16)
            asend[x, p] = made.reshape(4, 16, 128)
        for d in (2, 1, 3, 0):
            if d == e == 0:
                continue
            zh = (me.zh + d) % 4
            backs.add(asend.at[x, :, zh], arecv.at[mine], me.at(x=x, zh=zh))
    w_c.far_y()
    w_c_core = w_c.to_core(core, slice(None))
    arecv[mine] = asend[me.x, :, me.zh]
    backs.wait_recv()
    w_c_core.wait_recv()
    turn_back = (above == (along % 16) * 8 + along // 16).astype(F32).astype(BF16)
    attended = jnp.concatenate(
        [arecv[8 * h : 8 * h + 8, p].reshape(128, 128) for h in range(2) for p in range(3)], axis=1
    )
    attended = jnp.dot(turn_back, attended, preferred_element_type=F32).astype(BF16)
    for n in range(2):
        out[:, 384 * n : 384 * n + 384] = resid[:, 384 * n : 384 * n + 384] + jnp.dot(
            attended, wcbuf[n].reshape(768, 384), preferred_element_type=F32
        )
    links.finish()


def per_device(emb, trip, occ, wr, wq, wc, gain):
    vmem = pl.BlockSpec(memory_space=pltpu.VMEM)
    n = 52
    out = pl.pallas_call(
        layer_kernel,
        out_shape=jax.ShapeDtypeStruct((128, 768), F32),
        in_specs=[pl.BlockSpec(memory_space=pl.ANY)] * 7,
        out_specs=vmem,
        scratch_shapes=[
            pltpu.VMEM((16, 8, 768), BF16),
            pltpu.VMEM((16, 8, 768), BF16),
            pltpu.VMEM((4, 4, 8, 8, 384), BF16),
            pltpu.VMEM((4, 4, 8, 8, 384), BF16),
            pltpu.VMEM((4, 8, 8, 384), BF16),
            pltpu.VMEM((16, 12, 128), F32),
            pltpu.VMEM((16, 12, 128), F32),
            pltpu.VMEM((4, 12, 128), F32),
            pltpu.VMEM((16, 12, 128), F32),
            pltpu.VMEM((4, 8, 8, 384), BF16),
            pltpu.VMEM((4, 8, 8, 384), BF16),
            pltpu.VMEM((2, 4, 4, 6, 8, 384), BF16),
            pltpu.VMEM((2, 4, 4, 6, 8, 384), BF16),
            pltpu.VMEM((4, 4, 6, 8, 1152), BF16),
            pltpu.VMEM((4, 8, 128), F32),
            pltpu.VMEM((8, 8, 128), F32),
            pltpu.VMEM((128, 768), F32),
            pltpu.VMEM((2, 4, 16, 768), BF16),
            pltpu.VMEM((4, 16, 768), BF16),
            pltpu.VMEM((4, 2, 4, 16, 768), BF16),
            pltpu.VMEM((3, 512, 128), BF16),
            pltpu.VMEM((3, 512, 128), BF16),
            pltpu.VMEM((3, 256, 128), BF16),
            pltpu.VMEM((4, 3, 4, 16, 128), BF16),
            pltpu.VMEM((16, 3, 16, 128), BF16),
            pltpu.VMEM((8, 16), jnp.int32),
            pltpu.VMEM((16, 8, 768), BF16),
            pltpu.VMEM((768,), F32),
            pltpu.SemaphoreType.DMA((n,)),
            pltpu.SemaphoreType.DMA((n,)),
            pltpu.SemaphoreType.DMA((12,)),
        ],
        compiler_params=pltpu.CompilerParams(
            collective_id=1, has_side_effects=True, vmem_limit_bytes=56 * 1024 * 1024
        ),
        name="msa_layer",
    )(
        emb,
        trip,
        occ.T,
        wr.reshape(6, 8, 768),
        wq.reshape(6, 8, 2304),
        wc.reshape(6, 8, 768),
        gain,
    )
    return out.reshape(16, 8, 768)


def solution(mesh):
    both = P("seq", "col", None)
    return jax.shard_map(
        per_device,
        mesh=mesh,
        in_specs=(both, both, P("seq", "col"), P("col", None), P("col", None), P("col", None), P()),
        out_specs=both,
        check_vma=False,
    )
```
